128 devices in a mesh: row: 8 (over y, x_hi), col: 16 (over z, x_lo, core).
Axes of the slice: x: 4 (x_hi: 2, x_lo: 2; x = x_hi * 2 + x_lo), y: 4, z: 4, core: 2. Of those that a mesh axis runs over, the one named last changes fastest.
Arguments:
- orbitals: bfloat16 [1024, 20480], P(('row', 'col')), may hold values from -1.078125 to 1.078125
- targets: bfloat16 [128, 20480], P(('row', 'col')), may hold values from -0.0390625 to 0.0390625
- kernel: float32 [20480, 16, 1280], P('row', 'col'), may hold values from -6 to 6
- tile_owner: int32 [8, 16, 8, 16], P('row', None, None, 'col'), may hold values from 0 to 1, as said below
Outputs:
- applied: float32 [20480, 128], P(('row', 'col'))
The draws below stay inside these ranges and needn't reach their ends.
Inputs may be any that keep to these rules, and one draw needn't show every extreme that they name: For blocks q1 != q2, numbered as in the reference program, exactly one of tile_owner[r1, c1, r2, c2] and tile_owner[r2, c2, r1, c1] is 1 and the other 0; where q1 == q2 the entry is 1.
All inputs are finite; a program needn't handle non-finite values.
Results may differ from the reference program's by a relative error of at most 0.0003.
Values may be sent and summed in bfloat16 or wider, within the bound.
No kernel may reach another device: no remote copies, remote signals or barrier semaphores. Data moves between devices by JAX's collectives and lax.ppermute only.
A program may use at most 192 MiB of HBM per device.

```python
import jax
import jax.numpy as jnp
from jax import lax

NB = 1024
NT = 128
FB = 160
ROWS_GRID = 8
COLS_GRID = 16
NP = 20480
N_ROW = 8
N_COL = 16


def draw_tile_owner(key, part):
    key = jax.random.fold_in(key, 11)
    shape = (N_ROW, N_COL, N_ROW, N_COL)
    coins = jax.random.randint(key, shape, 0, 2).astype(jnp.int32)
    first = lax.broadcasted_iota(jnp.int32, shape, 0) * N_COL + lax.broadcasted_iota(jnp.int32, shape, 1)
    second = lax.broadcasted_iota(jnp.int32, shape, 2) * N_COL + lax.broadcasted_iota(jnp.int32, shape, 3)
    mirror = jnp.transpose(coins, (2, 3, 0, 1))
    ones = jnp.ones(shape, jnp.int32)
    return jnp.where(first < second, coins, jnp.where(first > second, 1 - mirror, ones)).astype(jnp.int32)


def steps_of(key, extent, pieces, smallest, largest):
    factor_of, own = 1.0, jax.random.fold_in(key, 6)
    for position, parts in pieces:
        heights = jnp.exp(jax.random.uniform(jax.random.fold_in(own, position), (parts,), jnp.float32, smallest / len(pieces), largest / len(pieces)))
        factor_of = factor_of * jnp.repeat(heights, extent[position] // parts).reshape([-1 if axis == position else 1 for axis in range(len(extent))])
    return factor_of


def normal_values(own_key, shape, deviation, reach, split=(), held_as=jnp.bfloat16):
    entries = jax.random.normal(own_key, shape, jnp.float32) * deviation
    if len(split) > 0:
        entries = steps_of(own_key, shape, split, -0.22, 0.18) * entries
    return jnp.clip(entries, min=-reach, max=reach).astype(held_as)


def setup_inputs(seed: int = 0) -> dict:
    key_of = jax.random.split(jax.random.key(seed), 5)
    return {
        "orbitals": normal_values(key_of[0], (NB, NP), 0.18, 1.078125, ((0, 128),)),
        "targets": normal_values(key_of[1], (NT, NP), NP ** -0.5, 0.0390625, ((0, 128),)),
        "kernel": normal_values(key_of[2], (NP, COLS_GRID, ROWS_GRID * FB), 1.0, 6.0, ((0, 8), (1, 16)), jnp.float32),
        "tile_owner": draw_tile_owner(jax.random.fold_in(key_of[4], 71), 0),
    }


def reference(orbitals, targets, kernel, tile_owner):
    blocks_all = ROWS_GRID * COLS_GRID
    points_all = blocks_all * FB
    stored = kernel.reshape(points_all, COLS_GRID, ROWS_GRID, FB).transpose(0, 2, 1, 3).reshape(points_all, points_all)
    owned_flags = tile_owner.reshape(blocks_all, blocks_all)
    target_cols = targets.astype(jnp.float32).T

    def one_block(index):
        start = index * FB
        rows_orb = lax.dynamic_slice_in_dim(orbitals, start, FB, 1)
        gram_rows = jnp.dot(rows_orb.T, orbitals, preferred_element_type=jnp.float32)
        direct = lax.dynamic_slice_in_dim(stored, start, FB, 0)
        mirror = lax.dynamic_slice_in_dim(stored, start, FB, 1).T
        flags = jnp.repeat(lax.dynamic_index_in_dim(owned_flags, index, 0, keepdims=False), FB)
        chosen = jnp.where(flags[None, :] == 1, direct, mirror)
        return jnp.dot(gram_rows * chosen, target_cols, precision=lax.Precision.HIGHEST)

    result = lax.map(one_block, jnp.arange(blocks_all, dtype=jnp.int32))
    return result.reshape(points_all, NT)
```

```python
import jax
import jax.numpy as jnp
from jax import lax
from jax.experimental import pallas as pl
from jax.experimental.pallas import tpu as pltpu
from jax.sharding import PartitionSpec as P

N_ROW, N_COL, FB = 8, 16, 160
ROW_PTS, COL_PTS = N_COL * FB, N_ROW * FB
AXES = ("row", "col")
Z_ORDER = (2, 1, 3, 0)
Y_ORDER = (0, 3, 1, 2)
TILE, CHUNK = 640, 256
BF, F32 = jnp.bfloat16, jnp.float32


def moved(y=0, xh=0, z=0, xl=0, k=0):
    pairs = []
    for i in range(N_ROW * N_COL):
        r, c = divmod(i, N_COL)
        r2 = ((r // 2 + y) % 4) * 2 + (r % 2 + xh) % 2
        c2 = ((c // 4 + z) % 4) * 4 + ((c // 2 % 2 + xl) % 2) * 2 + (c % 2 + k) % 2
        pairs.append((i, r2 * N_COL + c2))
    return pairs


def send(x, **steps):
    return lax.ppermute(x, AXES, moved(**steps))


def spread_kernel(xh_ref, own_ref, other_ref, out_ref):
    first = xh_ref[0] == 0
    own, other = own_ref[...], other_ref[...]
    both = jnp.concatenate([jnp.where(first, own, other), jnp.where(first, other, own)], axis=0)
    for c in range(N_COL):
        out_ref[c] = jnp.concatenate(
            [both[:, (r * N_COL + c) * FB : (r * N_COL + c + 1) * FB] for r in range(N_ROW)], axis=1
        )


def spread_points(own, other, xh):
    return pl.pallas_call(
        spread_kernel,
        out_shape=jax.ShapeDtypeStruct((N_COL, 16, COL_PTS), BF),
        in_specs=[
            pl.BlockSpec(memory_space=pltpu.SMEM),
            pl.BlockSpec(memory_space=pltpu.VMEM),
            pl.BlockSpec(memory_space=pltpu.VMEM),
        ],
        out_specs=pl.BlockSpec(memory_space=pltpu.VMEM),
        compiler_params=pltpu.CompilerParams(vmem_limit_bytes=32 * 2**20),
        name="spread",
    )(xh, own, other)


def nt(a, b):
    return lax.dot_general(a, b, (((1,), (1,)), ((), ())), preferred_element_type=F32)


def tile_kernel(
    me, rows, own, a_dn, b_dn, a_up, b_up, a_far, b_far, kern, owned, mirrored, tcol, trow,
    far_out, up_out, dn_out, own_out, c0, c1, c2, c3,
    cols, rows_t, row_acc, col_acc, col_turn, sems,
):
    s, n = pl.program_id(0), pl.program_id(1)
    y = me[1]

    @pl.when((s == 0) & (n == 0))
    def _():
        parts = ((own, 0, 16), (a_dn, 16, 8), (b_dn, 24, 8), (a_up, 32, 8), (b_up, 40, 8), (a_far, 48, 8), (b_far, 56, 8))
        copies = [
            pltpu.make_async_copy(src, cols.at[pl.ds(at, size)], sems.at[i])
            for i, (src, at, size) in enumerate(parts)
        ]
        for copy in copies:
            copy.start()
        for copy in copies:
            copy.wait()
        col_acc[...] = jnp.zeros_like(col_acc)

    @pl.when(n == 0)
    def _():
        for j, step in enumerate(Y_ORDER):
            part = rows[:, lax.rem(y + step, 4)].reshape(256, TILE)
            rows_t[:, 256 * j : 256 * (j + 1)] = part.T
        row_acc[...] = jnp.zeros_like(row_acc)

    at = pl.ds(pl.multiple_of(n * CHUNK, CHUNK), CHUNK)
    gram = jnp.dot(rows_t[...], cols[:, :, at].reshape(1024, CHUNK), preferred_element_type=F32)

    def spread(ref):
        return jnp.concatenate([jnp.broadcast_to(ref[0, i : i + 1, :], (FB, CHUNK)) for i in range(4)], axis=0)

    weighted = gram * kern[...] * spread(owned)
    high = weighted.astype(BF)
    low = (weighted - high.astype(F32)).astype(BF)
    row_acc[...] += nt(high, tcol[...]) + nt(low, tcol[...])
    keep = spread(mirrored).astype(BF)
    col_acc[:, at] += jnp.dot(trow[...], high * keep, preferred_element_type=F32) + jnp.dot(
        trow[...], low * keep, preferred_element_type=F32
    )

    for i, out in enumerate((far_out, up_out, dn_out, own_out)):

        @pl.when((s == i) & (n == 4))
        def _(out=out):
            out[...] = row_acc[...]

    @pl.when((s == 3) & (n == 4))
    def _():
        turned = col_acc[...].T
        for q in range(4):
            col_turn[q] = turned[q * 320 : (q + 1) * 320]
        for d, out in enumerate((c0, c1, c2, c3)):
            out[...] = col_turn[lax.rem(y + d, 4)]


def tile_products(me, rows, col_parts, kern, owned, mirrored, tcol, trow):
    def ztile(s, me):
        step = jnp.where(s == 0, 2, jnp.where(s == 1, 1, jnp.where(s == 2, 3, 0)))
        return lax.rem(me[0] + step, 4)

    hold = lambda s, n, me: (0, 0)
    spec = pltpu.PrefetchScalarGridSpec(
        num_scalar_prefetch=1,
        grid=(4, 5),
        in_specs=[pl.BlockSpec((16, 4, 16, TILE), lambda s, n, me: (0, 0, 0, ztile(s, me)))]
        + [pl.BlockSpec(memory_space=pl.ANY)] * 7
        + [
            pl.BlockSpec((TILE, CHUNK), lambda s, n, me: (ztile(s, me), n)),
            pl.BlockSpec((1, 4, CHUNK), lambda s, n, me: (ztile(s, me), 0, n)),
            pl.BlockSpec((1, 4, CHUNK), lambda s, n, me: (ztile(s, me), 0, n)),
            pl.BlockSpec((128, CHUNK), lambda s, n, me: (0, n)),
            pl.BlockSpec((128, TILE), lambda s, n, me: (0, ztile(s, me))),
        ],
        out_specs=[pl.BlockSpec((TILE, 128), hold)] * 4 + [pl.BlockSpec((320, 128), hold)] * 4,
        scratch_shapes=[
            pltpu.VMEM((64, 16, COL_PTS), BF),
            pltpu.VMEM((TILE, 1024), BF),
            pltpu.VMEM((TILE, 128), F32),
            pltpu.VMEM((128, COL_PTS), F32),
            pltpu.VMEM((4, 320, 128), F32),
            pltpu.SemaphoreType.DMA((7,)),
        ],
    )
    return pl.pallas_call(
        tile_kernel,
        grid_spec=spec,
        out_shape=[jax.ShapeDtypeStruct((TILE, 128), F32)] * 4 + [jax.ShapeDtypeStruct((320, 128), F32)] * 4,
        compiler_params=pltpu.CompilerParams(
            vmem_limit_bytes=40 * 2**20, dimension_semantics=("arbitrary", "arbitrary")
        ),
        cost_estimate=pl.CostEstimate(flops=10_000_000_000, bytes_accessed=24_000_000, transcendentals=0),
        name="tile_products",
    )(me, rows, *col_parts, kern, owned, mirrored, tcol, trow)


def pick(blocks, index):
    return lax.dynamic_index_in_dim(blocks, index, 0, keepdims=False)


def local(orbitals, targets, kernel, tile_owner):
    r, c = lax.axis_index("row"), lax.axis_index("col")
    y, xh = r // 2, r % 2
    z, xl, k = c // 4, c // 2 % 2, c % 2

    other = send(orbitals, xh=1)
    row_part = lax.all_to_all(orbitals, "row", split_axis=1, concat_axis=0, tiled=True)
    rows = lax.all_gather(row_part, "col", axis=0, tiled=True).reshape(16, 4, 16, ROW_PTS)

    col_part = spread_points(orbitals, other, xh.reshape(1))
    own = lax.all_to_all(col_part, "col", split_axis=0, concat_axis=0, tiled=True)
    half_a, half_b = own[:8], own[8:]
    a_dn, b_up = send(half_a, y=1), send(half_b, y=3)
    b_dn, a_up = send(half_b, y=1), send(half_a, y=3)
    a_far, b_far = send(a_dn, y=1), send(b_up, y=3)

    trow = lax.all_to_all(targets, "row", split_axis=1, concat_axis=0, tiled=True)
    trow = lax.all_gather(trow, "col", axis=0, tiled=True)
    trow = trow.reshape(N_COL, N_ROW, ROW_PTS).transpose(1, 0, 2).reshape(128, ROW_PTS)
    tcol = targets.reshape(N_ROW, N_COL, FB).transpose(1, 0, 2).reshape(N_COL, COL_PTS)
    tcol = lax.all_to_all(tcol, "col", split_axis=0, concat_axis=0, tiled=True)
    tcol = lax.all_gather(tcol, "row", axis=0, tiled=True)

    flags = tile_owner.reshape(N_COL, N_ROW).astype(F32)
    here = (lax.broadcasted_iota(jnp.int32, flags.shape, 0) == c) & (
        lax.broadcasted_iota(jnp.int32, flags.shape, 1) == r
    )
    owned = jnp.repeat(flags, FB, axis=1).reshape(4, 4, COL_PTS)
    mirrored = jnp.repeat(jnp.where(here, 0.0, flags), FB, axis=1).reshape(4, 4, COL_PTS)

    far, up, dn, mine, c0, c1, c2, c3 = tile_products(
        jnp.stack([z, y]).astype(jnp.int32),
        rows, (own, a_dn, b_dn, a_up, b_up, a_far, b_far),
        kernel.reshape(ROW_PTS, COL_PTS), owned, mirrored, tcol, trow,
    )
    row_sum = mine + send(far, z=2) + send(up, z=1) + send(dn, z=3)
    col_sum = c0 + send(c2, y=2) + send(c1, y=1) + send(c3, y=3)

    by_core = row_sum.reshape(2, 2, FB, 128).transpose(1, 0, 2, 3)
    row_sum = pick(by_core, k) + send(pick(by_core, 1 - k), k=1)
    row_share = pick(row_sum, xl) + send(pick(row_sum, 1 - xl), xl=1)
    col_sum = col_sum.reshape(2, FB, 128)
    col_share = pick(col_sum, xh) + send(pick(col_sum, 1 - xh), xh=1)
    return row_share + col_share


def solution(mesh):
    in_specs = (
        P(("row", "col"), None),
        P(("row", "col"), None),
        P("row", "col", None),
        P("row", None, None, "col"),
    )
    out_specs = P(("row", "col"), None)
    return jax.shard_map(local, mesh=mesh, in_specs=in_specs, out_specs=out_specs, check_vma=False)
```

```python
import itertools

import jax
import jax.numpy as jnp
from jax import lax
from jax.experimental import pallas as pl
from jax.experimental.pallas import tpu as pltpu
from jax.sharding import PartitionSpec as P

N_ROW, N_COL, FB, NB, NT = 8, 16, 160, 1024, 128
DEVICES = N_ROW * N_COL
ROW_PTS, COL_PTS = N_COL * FB, N_ROW * FB
WIDE = NB + NT
AXES = ("row", "col")
PARTS = {"y": 4, "xh": 2, "z": 4, "xl": 2, "k": 2}
TILE = 4 * FB
BF, F32 = jnp.bfloat16, jnp.float32


def index_of(y, xh, z, xl, k):
    return (y * 2 + xh) * N_COL + z * 4 + xl * 2 + k


def moved(**steps):
    pairs = []
    for at in itertools.product(*map(range, PARTS.values())):
        to = [(a + steps.get(name, 0)) % size for a, (name, size) in zip(at, PARTS.items())]
        pairs.append((index_of(*at), index_of(*to)))
    return pairs


def groups(*names):
    found = {}
    for at in itertools.product(*map(range, PARTS.values())):
        rest = tuple(a for a, name in zip(at, PARTS) if name not in names)
        found.setdefault(rest, []).append(index_of(*at))
    return list(found.values())


def send(x, **steps):
    return lax.ppermute(x, AXES, moved(**steps))


def nn(a, b):
    return jnp.dot(a, b, preferred_element_type=F32)


def nt(a, b):
    return lax.dot_general(a, b, (((1,), (1,)), ((), ())), preferred_element_type=F32)


def tn(a, b):
    return lax.dot_general(a, b, (((0,), (0,)), ((), ())), preferred_element_type=F32)


def pack_kernel(orb, tgt, out):
    row = lax.broadcasted_iota(jnp.int32, (8, 96), 0)
    for pair in range(DEVICES // 2):
        blocks = []
        for q in (2 * pair, 2 * pair + 1):
            head = jnp.broadcast_to(tgt[q : q + 1, :96], (8, 96))
            tail = jnp.broadcast_to(tgt[q : q + 1, 64:], (8, 96))
            extra = jnp.where(row == 0, head, tail)
            blocks.append(jnp.concatenate([orb[:, q * FB : (q + 1) * FB].astype(F32), extra], axis=1))
        out[16 * pair : 16 * (pair + 1), :] = jnp.concatenate(blocks, axis=0).astype(BF)


def pack(orbitals, targets):
    return pl.pallas_call(
        pack_kernel,
        out_shape=jax.ShapeDtypeStruct((DEVICES * 8, 256), BF),
        compiler_params=pltpu.CompilerParams(vmem_limit_bytes=32 * 2**20),
        name="pack",
    )(orbitals, targets.astype(F32).reshape(DEVICES, FB))


def unpack_kernel(packed, out):
    out[:, :NB] = packed[:, :FB].T
    source = lax.broadcasted_iota(jnp.int32, (NB, NT), 0)
    target = lax.broadcasted_iota(jnp.int32, (NB, NT), 1)
    first = jnp.where(source == 8 * target, 1.0, 0.0).astype(BF)
    second = jnp.where(source == 8 * target + 1, 1.0, 0.0).astype(BF)
    heads = tn(packed[...], first)
    tails = tn(packed[...], second)
    out[:96, NB:] = heads[FB:].astype(BF)
    out[96:, NB:] = tails[FB + 32 :].astype(BF)


def unpack(packed):
    return pl.pallas_call(
        unpack_kernel,
        out_shape=jax.ShapeDtypeStruct((FB, WIDE), BF),
        compiler_params=pltpu.CompilerParams(vmem_limit_bytes=32 * 2**20),
        name="unpack",
    )(packed)


def tile_step(me, rows, pair, down, up, far_own, far_other, kern, owned, mirrored, cols, sems, col_acc, col_start):
    y, xh = me[1], me[2]

    @pl.when(pl.program_id(0) == 0)
    def _():
        def block(y_step, side):
            return lax.rem(y + y_step, 4) * 2 + lax.rem(xh + side, 2)

        pieces = [(ref.at[pl.ds(FB * side, FB)], block(step, side)) for ref, step in ((pair, 0), (down, 3), (up, 1)) for side in (0, 1)]
        pieces += [(far_own, block(2, 0)), (far_other, block(2, 1))]
        copies = [pltpu.make_async_copy(src, cols.at[at], sems.at[i]) for i, (src, at) in enumerate(pieces)]
        for copy in copies:
            copy.start()
        col_start()
        for copy in copies:
            copy.wait()

    row_wide = rows[...].reshape(TILE, WIDE)
    col_wide = cols[...].reshape(COL_PTS, WIDE)
    gram = nt(row_wide[:, :NB], col_wide[:, :NB])
    stored = jnp.concatenate(
        [
            jnp.concatenate([kern[b, 0, pl.ds(j, FB, stride=COL_PTS // 128), :] for j in range(COL_PTS // 128)], axis=1)
            for b in range(4)
        ],
        axis=0,
    )

    def spread(ref):
        return jnp.concatenate([jnp.broadcast_to(ref[b, 0], (FB, COL_PTS)) for b in range(4)], axis=0)

    weighted = gram * stored * spread(owned)
    high = weighted.astype(BF)
    low = (weighted - high.astype(F32)).astype(BF)
    row_sum = nn(high, col_wide[:, NB:]) + nn(low, col_wide[:, NB:])
    keep = spread(mirrored).astype(BF)
    col_sum = tn(high * keep, row_wide[:, NB:]) + tn(low * keep, row_wide[:, NB:])
    col_acc[...] += col_sum.reshape(col_acc.shape)
    return row_sum.reshape(4, FB, NT)


def first_kernel(me, *refs):
    ins, (row_out, col_out), (cols, sems) = refs[:9], refs[9:11], refs[11:]

    def start():
        col_out[...] = jnp.zeros_like(col_out)

    row_out[...] = tile_step(me, *ins, cols, sems, col_out, start)


def second_kernel(me, *refs):
    ins, col_in, outs, (cols, sems, col_acc) = refs[:9], refs[9], refs[10:15], refs[15:]

    def start():
        col_acc[...] = col_in[...]

    outs[0][...] = tile_step(me, *ins, cols, sems, col_acc, start)

    @pl.when(pl.program_id(0) == 1)
    def _():
        for step in range(4):
            outs[1 + step][...] = col_acc[lax.rem(me[1] + step, 4)]


def tile_call(me, rows, col_parts, kern, owned, mirrored, col_in=None):
    second = col_in is not None
    in_specs = [pl.BlockSpec((4, 1, FB, WIDE), lambda g, me: (g, me[0], 0, 0))]
    in_specs += [pl.BlockSpec(memory_space=pltpu.HBM)] * len(col_parts)
    in_specs += [pl.BlockSpec((4, 1, FB * COL_PTS // 128, 128), lambda g, me: (g, me[0], 0, 0))]
    in_specs += [pl.BlockSpec((4, 1, 1, COL_PTS), lambda g, me: (g, me[0], 0, 0))] * 2
    row_out = jax.ShapeDtypeStruct((8, FB, NT), F32)
    row_spec = pl.BlockSpec((4, FB, NT), lambda g, me: (g, 0, 0))
    whole = pl.BlockSpec((4, 2 * FB, NT), lambda g, me: (0, 0, 0))
    scratch = [pltpu.VMEM((N_ROW, FB, WIDE), BF), pltpu.SemaphoreType.DMA((8,))]
    args = [me, rows, *col_parts, kern, owned, mirrored]
    if second:
        in_specs += [whole]
        args += [col_in]
        out_shape = [row_out] + [jax.ShapeDtypeStruct((2 * FB, NT), F32)] * 4
        out_specs = [row_spec] + [pl.BlockSpec((2 * FB, NT), lambda g, me: (0, 0))] * 4
        scratch += [pltpu.VMEM((4, 2 * FB, NT), F32)]
    else:
        out_shape = [row_out, jax.ShapeDtypeStruct((4, 2 * FB, NT), F32)]
        out_specs = [row_spec, whole]
    return pl.pallas_call(
        second_kernel if second else first_kernel,
        grid_spec=pltpu.PrefetchScalarGridSpec(
            num_scalar_prefetch=1, grid=(2,), in_specs=in_specs, out_specs=out_specs, scratch_shapes=scratch
        ),
        out_shape=out_shape,
        compiler_params=pltpu.CompilerParams(vmem_limit_bytes=56 * 2**20, dimension_semantics=("arbitrary",)),
        cost_estimate=pl.CostEstimate(flops=5_000_000_000, bytes_accessed=13_000_000, transcendentals=0),
        name="tiles_of_own_core" if second else "tiles_of_other_core",
    )(*args)


def local(orbitals, targets, kernel, tile_owner):
    r, c = lax.axis_index("row"), lax.axis_index("col")
    y, xh, k = r // 2, r % 2, c % 2

    packed = pack(orbitals, targets).reshape(DEVICES, 8, 256)
    packed = lax.all_to_all(packed, AXES, split_axis=0, concat_axis=0, tiled=True)
    own = unpack(packed.reshape(DEVICES * 8, 256))

    rows = lax.all_gather(own, "col", axis=0, tiled=True).reshape(8, 2, FB, WIDE)
    pair = jnp.concatenate([own, send(own, xh=1)], axis=0)
    down, up = send(pair, y=1), send(pair, y=3)
    far_own, far_other = send(down[:FB], y=1), send(up[FB:], y=3)
    col_parts = (pair, down, up, far_own, far_other)

    flags = tile_owner.reshape(N_COL, N_ROW).astype(F32)
    here = (lax.broadcasted_iota(jnp.int32, flags.shape, 0) == c) & (
        lax.broadcasted_iota(jnp.int32, flags.shape, 1) == r
    )
    owned = jnp.repeat(flags, FB, axis=1).reshape(8, 2, 1, COL_PTS)
    mirrored = jnp.repeat(jnp.where(here, 0.0, flags), FB, axis=1).reshape(8, 2, 1, COL_PTS)
    kern = kernel.reshape(8, 2, FB * COL_PTS // 128, 128)

    def place(core):
        return jnp.stack([core, y, xh]).astype(jnp.int32)

    row_other, col_part = tile_call(place(1 - k), rows, col_parts, kern, owned, mirrored)
    row_own, c0, c1, c2, c3 = tile_call(place(k), rows, col_parts, kern, owned, mirrored, col_part)

    row_sum = row_own + send(row_other, k=1)
    row_share = lax.all_to_all(
        row_sum, AXES, split_axis=0, concat_axis=0, axis_index_groups=groups("z", "xl"), tiled=True
    ).sum(axis=0)
    col_sum = (c0 + send(c1, y=1) + send(c2, y=2) + send(c3, y=3)).reshape(2, FB, NT)
    mine = lax.dynamic_index_in_dim(col_sum, xh, 0, keepdims=False)
    theirs = lax.dynamic_index_in_dim(col_sum, 1 - xh, 0, keepdims=False)
    return row_share + mine + send(theirs, xh=1)


def solution(mesh):
    in_specs = (
        P(("row", "col"), None),
        P(("row", "col"), None),
        P("row", "col", None),
        P("row", None, None, "col"),
    )
    out_specs = P(("row", "col"), None)
    return jax.shard_map(local, mesh=mesh, in_specs=in_specs, out_specs=out_specs, check_vma=False)
```

```python
import functools
import itertools

import jax
import jax.numpy as jnp
from jax import lax
from jax.experimental import pallas as pl
from jax.experimental.pallas import tpu as pltpu
from jax.sharding import PartitionSpec as P

N_ROW, N_COL, FB, NB, NT = 8, 16, 160, 1024, 128
DEVICES = N_ROW * N_COL
ROW_PTS, COL_PTS = N_COL * FB, N_ROW * FB
WIDE = NB + NT
AXES = ("row", "col")
PARTS = {"y": 4, "xh": 2, "z": 4, "xl": 2, "k": 2}
TILE = 4 * FB
BF, F32 = jnp.bfloat16, jnp.float32


def index_of(y, xh, z, xl, k):
    return (y * 2 + xh) * N_COL + z * 4 + xl * 2 + k


def moved(**steps):
    pairs = []
    for at in itertools.product(*map(range, PARTS.values())):
        to = [(a + steps.get(name, 0)) % size for a, (name, size) in zip(at, PARTS.items())]
        pairs.append((index_of(*at), index_of(*to)))
    return pairs


def send(x, **steps):
    return lax.ppermute(x, AXES, moved(**steps))


def nn(a, b):
    return jnp.dot(a, b, preferred_element_type=F32)


def nt(a, b):
    return lax.dot_general(a, b, (((1,), (1,)), ((), ())), preferred_element_type=F32)


def tn(a, b):
    return lax.dot_general(a, b, (((0,), (0,)), ((), ())), preferred_element_type=F32)


def pack_kernel(orb, tgt, out):
    row = lax.broadcasted_iota(jnp.int32, (8, FB), 0)
    for pair in range(DEVICES // 2):
        blocks = []
        for q in (2 * pair, 2 * pair + 1):
            sources = (q, q ^ 16, q ^ 2)
            extra = jnp.where(
                row == 0,
                tgt[sources[0] : sources[0] + 1, :],
                jnp.where(row == 1, tgt[sources[1] : sources[1] + 1, :], tgt[sources[2] : sources[2] + 1, :]),
            )
            pieces = [orb[:, s * FB : (s + 1) * FB].astype(F32) for s in sources]
            blocks.append(jnp.concatenate([*pieces, extra], axis=1))
        out[16 * pair : 16 * (pair + 1), :] = jnp.concatenate(blocks, axis=0).astype(BF)


def pack(orbitals, targets):
    return pl.pallas_call(
        pack_kernel,
        out_shape=jax.ShapeDtypeStruct((DEVICES * 8, 4 * FB), BF),
        compiler_params=pltpu.CompilerParams(vmem_limit_bytes=32 * 2**20),
        name="pack",
    )(orbitals, targets.astype(F32).reshape(DEVICES, FB))


def unpack_kernel(packed, cols, rows):
    turned = packed[:, : 3 * FB].T
    cols[: FB, :NB] = turned[:FB]
    cols[FB:, :NB] = turned[FB : 2 * FB]
    rows[:FB, :NB] = turned[:FB]
    rows[FB:, :NB] = turned[2 * FB :]
    source = lax.broadcasted_iota(jnp.int32, (NB, NT), 0)
    target = lax.broadcasted_iota(jnp.int32, (NB, NT), 1)
    mine, col_side, row_side = (
        tn(packed[...], jnp.where(source == 8 * target + i, 1.0, 0.0).astype(BF))[3 * FB :].astype(BF) for i in range(3)
    )
    cols[:FB, NB:] = mine
    cols[FB:, NB:] = col_side
    rows[:FB, NB:] = mine
    rows[FB:, NB:] = row_side


def unpack(packed):
    return pl.pallas_call(
        unpack_kernel,
        out_shape=[jax.ShapeDtypeStruct((2 * FB, WIDE), BF)] * 2,
        compiler_params=pltpu.CompilerParams(vmem_limit_bytes=32 * 2**20),
        name="unpack",
    )(packed)


def tile_kernel(z_steps, me, *refs):
    tiles = len(z_steps)
    far = tiles == 1
    n_rows = 4 if far else 2 * tiles
    row_refs, refs = refs[:n_rows], refs[n_rows:]
    (pair, down, up, far_own, far_other, kern, owned, mirrored), refs = refs[:8], refs[8:]
    if far:
        col_in, refs = refs[0], refs[1:]
    row_own, row_other, col_out, cols, rows, stored, sems = refs
    y, xh, z, xl, k = (me[i] for i in range(5))

    def block(y_step, side):
        return lax.rem(y + y_step, 4) * 2 + lax.rem(xh + side, 2)

    count = [0]

    def start(src, dst):
        copy = pltpu.make_async_copy(src, dst, sems.at[count[0]])
        count[0] += 1
        copy.start()
        return copy

    def tile_copies(t):
        z_at = lax.rem(z + z_steps[t], 4)
        found = []
        if far:
            found += [start(row_refs[b], rows.at[0, b]) for b in range(4)]
        else:
            found += [start(row_refs[2 * t + b], rows.at[t, pl.ds(2 * b, 2)]) for b in range(2)]
        for b in range(4):
            found.append(start(kern.at[z_at, lax.rem(xl + b % 2, 2), lax.rem(k + b // 2, 2)], stored.at[t, b]))
        return found

    pieces = [(ref.at[side], block(step, side)) for ref, step in ((pair, 0), (down, 3), (up, 1)) for side in (0, 1)]
    pieces += [(far_own, block(2, 0)), (far_other, block(2, 1))]
    col_copies = [start(src, cols.at[at]) for src, at in pieces]
    row_copies = [tile_copies(t) for t in range(tiles)]
    if far:
        col_out[...] = col_in[...]
    else:
        col_out[...] = jnp.zeros_like(col_out)
    for copy in col_copies:
        copy.wait()
    col_wide = cols[...].reshape(COL_PTS, WIDE)

    for t in range(tiles):
        z_at = lax.rem(z + z_steps[t], 4)
        for copy in row_copies[t]:
            copy.wait()
        row_wide = rows[t].reshape(TILE, WIDE)
        gram = nt(row_wide[:, :NB], col_wide[:, :NB])
        chunks = COL_PTS // 128
        values = jnp.concatenate(
            [
                jnp.concatenate([stored[t, b, pl.ds(j, FB, stride=chunks), :] for j in range(chunks)], axis=1)
                for b in range(4)
            ],
            axis=0,
        )

        def spread(ref):
            return jnp.concatenate(
                [
                    jnp.broadcast_to(ref[z_at, lax.rem(xl + b % 2, 2), lax.rem(k + b // 2, 2)], (FB, COL_PTS))
                    for b in range(4)
                ],
                axis=0,
            )

        weighted = gram * values * spread(owned)
        high = weighted.astype(BF)
        low = (weighted - high.astype(F32)).astype(BF)
        row_sum = nn(high, col_wide[:, NB:]) + nn(low, col_wide[:, NB:])
        keep = spread(mirrored).astype(BF)
        col_sum = tn(high * keep, row_wide[:, NB:]) + tn(low * keep, row_wide[:, NB:])
        col_out[...] += col_sum.reshape(col_out.shape)
        row_own[t] = row_sum[: 2 * FB]
        row_other[t] = row_sum[2 * FB :]


def tile_call(z_steps, me, rows, col_parts, kern, owned, mirrored, col_in=None):
    tiles = len(z_steps)
    vmem = pl.BlockSpec(memory_space=pltpu.VMEM)
    hbm = pl.BlockSpec(memory_space=pltpu.HBM)
    in_specs = [pl.BlockSpec(memory_space=pltpu.SMEM)] + [hbm] * (len(rows) + len(col_parts) + 1) + [vmem] * 2
    args = [me, *rows, *col_parts, kern, owned, mirrored]
    if col_in is not None:
        in_specs.append(vmem)
        args.append(col_in)
    copies = 8 + len(rows) + 4 * tiles
    return pl.pallas_call(
        functools.partial(tile_kernel, z_steps),
        in_specs=in_specs,
        out_specs=[vmem] * 3,
        out_shape=[jax.ShapeDtypeStruct((tiles, 2 * FB, NT), F32)] * 2 + [jax.ShapeDtypeStruct((N_ROW, FB, NT), F32)],
        scratch_shapes=[
            pltpu.VMEM((N_ROW, FB, WIDE), BF),
            pltpu.VMEM((tiles, 4, FB, WIDE), BF),
            pltpu.VMEM((tiles, 4, FB * COL_PTS // 128, 128), F32),
            pltpu.SemaphoreType.DMA((copies,)),
        ],
        compiler_params=pltpu.CompilerParams(vmem_limit_bytes=(46 if tiles > 1 else 32) * 2**20),
        cost_estimate=pl.CostEstimate(
            flops=2_600_000_000 * tiles, bytes_accessed=5_000_000 * tiles, transcendentals=0
        ),
        name="near_tiles" if tiles > 1 else "far_tile",
    )(*args)


def halves(pair):
    return pair.reshape(2, FB, pair.shape[-1])


def local(orbitals, targets, kernel, tile_owner):
    r, c = lax.axis_index("row"), lax.axis_index("col")
    me = jnp.stack([r // 2, r % 2, c // 4, c // 2 % 2, c % 2]).astype(jnp.int32)

    packed = pack(orbitals, targets).reshape(DEVICES, 8, 4 * FB)
    packed = lax.all_to_all(packed, AXES, split_axis=0, concat_axis=0, tiled=True)
    pair_y, pair_z = unpack(packed.reshape(DEVICES * 8, 4 * FB))

    y_down, y_up = send(pair_y, y=1), send(pair_y, y=3)
    z_down, z_up = send(pair_z, z=1), send(pair_z, z=3)
    y_far, y_far_other = send(y_down[:FB], y=1), send(y_up[FB:], y=3)
    z_far, z_far_other = send(z_down[:FB], z=1), send(z_up[FB:], z=3)
    col_parts = (halves(pair_y), halves(y_down), halves(y_up), y_far, y_far_other)
    near_rows = [halves(part) for own in (pair_z, z_up, z_down) for part in (own, send(own, k=1))]
    far_rows = [z_far, z_far_other, send(z_far, k=1), send(z_far_other, k=1)]

    flags = tile_owner.reshape(N_COL, N_ROW).astype(F32)
    here = (lax.broadcasted_iota(jnp.int32, flags.shape, 0) == c) & (
        lax.broadcasted_iota(jnp.int32, flags.shape, 1) == r
    )
    owned = jnp.repeat(flags, FB, axis=1).reshape(4, 2, 2, 1, COL_PTS)
    mirrored = jnp.repeat(jnp.where(here, 0.0, flags), FB, axis=1).reshape(4, 2, 2, 1, COL_PTS)
    kern = kernel.reshape(4, 2, 2, FB * COL_PTS // 128, 128)

    near_own, near_other, col_part = tile_call((0, 1, 3), me, near_rows, col_parts, kern, owned, mirrored)
    far_own, far_other, col_sum = tile_call((2,), me, far_rows, col_parts, kern, owned, mirrored, col_part)

    near = near_own + send(near_other, k=1)
    far = far_own + send(far_other, k=1)
    row_sum = near[0] + send(near[1], z=1) + send(near[2], z=3) + send(far[0], z=2)
    row_share = row_sum[:FB] + send(row_sum[FB:], xl=1)
    col_share = lax.all_to_all(col_sum, "row", split_axis=0, concat_axis=0, tiled=True).sum(axis=0)
    return row_share + col_share


def solution(mesh):
    in_specs = (
        P(("row", "col"), None),
        P(("row", "col"), None),
        P("row", "col", None),
        P("row", None, None, "col"),
    )
    out_specs = P(("row", "col"), None)
    return jax.shard_map(local, mesh=mesh, in_specs=in_specs, out_specs=out_specs, check_vma=False)
```

```python
import itertools

import jax
import jax.numpy as jnp
from jax import lax
from jax.experimental import pallas as pl
from jax.experimental.pallas import tpu as pltpu
from jax.sharding import PartitionSpec as P

N_ROW, N_COL, FB, NB, NT = 8, 16, 160, 1024, 128
DEVICES = N_ROW * N_COL
ROW_PTS, COL_PTS = N_COL * FB, N_ROW * FB
WIDE = NB + NT
AXES = ("row", "col")
PARTS = {"y": 4, "xh": 2, "z": 4, "xl": 2, "k": 2}
TILE = 4 * FB
POINTS = 8 * FB
SENT = 2944
BF, F32 = jnp.bfloat16, jnp.float32


def index_of(y, xh, z, xl, k):
    return (y * 2 + xh) * N_COL + z * 4 + xl * 2 + k


def moved(**steps):
    pairs = []
    for at in itertools.product(*map(range, PARTS.values())):
        to = [(a + steps.get(name, 0)) % size for a, (name, size) in zip(at, PARTS.items())]
        pairs.append((index_of(*at), index_of(*to)))
    return pairs


def send(x, **steps):
    return lax.ppermute(x, AXES, moved(**steps))


def nn(a, b):
    return jnp.dot(a, b, preferred_element_type=F32)


def nt(a, b):
    return lax.dot_general(a, b, (((1,), (1,)), ((), ())), preferred_element_type=F32)


def tn(a, b):
    return lax.dot_general(a, b, (((0,), (0,)), ((), ())), preferred_element_type=F32)


def pack_kernel(orb, tgt, out, split):
    split[0] = tgt[:, :128]
    split[1, :, : FB - 128] = tgt[:, 128:]

    def joined(blocks):
        return jnp.concatenate([orb[:, q * FB : (q + 1) * FB].astype(F32) for q in blocks], axis=1)

    def paired(first, second):
        return jnp.concatenate([first, second], axis=0).astype(BF)

    def tgt_rows(start, stride):
        at = pl.ds(start, 8, stride=stride)
        return jnp.concatenate([split[0, at, :], split[1, at, :][:, : FB - 128]], axis=1)

    fill = jnp.zeros((8, SENT - 2 * POINTS - 2 * FB), F32)
    row_part = [paired(*(joined(range(r * N_COL + 1 - k, (r + 1) * N_COL, 2)) for k in (0, 1))) for r in range(N_ROW)]
    for half in range(N_COL // 2):
        col_part = paired(*(joined(range(2 * half + k, DEVICES, N_COL)) for k in (0, 1)))
        for r in range(N_ROW):
            at = pl.ds((r * N_COL + 2 * half) * 8, 16)
            out[at, :POINTS] = col_part
            out[at, POINTS : 2 * POINTS] = row_part[r]
            out[at, 2 * POINTS :] = paired(
                *(
                    jnp.concatenate([tgt_rows(2 * half + k, N_COL), tgt_rows(r * N_COL + 1 - k, 2), fill], axis=1)
                    for k in (0, 1)
                )
            )


def pack(orbitals, targets):
    return pl.pallas_call(
        pack_kernel,
        out_shape=jax.ShapeDtypeStruct((DEVICES * 8, SENT), BF),
        scratch_shapes=[pltpu.VMEM((2, DEVICES, 128), F32)],
        compiler_params=pltpu.CompilerParams(vmem_limit_bytes=40 * 2**20),
        name="pack",
    )(orbitals, targets.astype(F32).reshape(DEVICES, FB))


def unpack_kernel(packed, rows, tcol):
    source = lax.broadcasted_iota(jnp.int32, (NB, NB), 0)
    target = lax.broadcasted_iota(jnp.int32, (NB, NB), 1)
    order = jnp.where(source == lax.rem(target, NT) * 8 + target // NT, 1.0, 0.0).astype(BF)
    tgt = tn(packed[:, 2 * POINTS :], order).astype(BF)
    turned = packed[:, POINTS : 2 * POINTS].T
    for b in range(8):
        at = slice(b * NT, (b + 1) * NT)
        tcol[b * FB : (b + 1) * FB, :] = tgt[:FB, at]
        rows[b, :, :NB] = turned[b * FB : (b + 1) * FB]
        rows[b, :, NB:] = tgt[FB : 2 * FB, at]


def unpack(packed):
    return pl.pallas_call(
        unpack_kernel,
        out_shape=[jax.ShapeDtypeStruct((8, FB, WIDE), BF), jax.ShapeDtypeStruct((POINTS, NT), BF)],
        compiler_params=pltpu.CompilerParams(vmem_limit_bytes=40 * 2**20),
        name="unpack",
    )(packed)


def tile_kernel(me, rows, packed, tcol, kern, owned, mirrored, *refs):
    col_in, refs = (refs[0], refs[1:]) if len(refs) == 7 else (None, refs)
    row_out, col_out, cols, row_buf, stored, sems = refs
    z, xl, core = me[0], me[1], me[2]

    def place(t, b):
        return lax.rem(z + 2 * t + b // 2, 4), lax.rem(xl + b % 2, 2)

    count = [0]

    def start(src, dst):
        copy = pltpu.make_async_copy(src, dst, sems.at[count[0]])
        count[0] += 1
        copy.start()
        return copy

    col_copy = start(packed.at[:, pl.ds(0, POINTS)], cols)
    row_copies, kern_copies = [], []
    for t in range(2):
        spots = [place(t, b) for b in range(4)]
        row_copies.append([start(rows.at[zz * 2 + xx], row_buf.at[t, b]) for b, (zz, xx) in enumerate(spots)])
        kern_copies.append([start(kern.at[zz, xx, core], stored.at[t, b]) for b, (zz, xx) in enumerate(spots)])
    if col_in is None:
        col_out[...] = jnp.zeros_like(col_out)
    else:
        col_out[...] = col_in[...]
    col_copy.wait()

    for t in range(2):
        for copy in row_copies[t]:
            copy.wait()
        row_wide = row_buf[t].reshape(TILE, WIDE)
        gram = nn(row_wide[:, :NB], cols[...])
        for copy in kern_copies[t]:
            copy.wait()
        chunks = COL_PTS // 128
        values = jnp.concatenate(
            [
                jnp.concatenate([stored[t, b, pl.ds(j, FB, stride=chunks), :] for j in range(chunks)], axis=1)
                for b in range(4)
            ],
            axis=0,
        )

        def spread(ref):
            return jnp.concatenate(
                [jnp.broadcast_to(ref[(*place(t, b), core)], (FB, COL_PTS)) for b in range(4)], axis=0
            )

        weighted = gram * values * spread(owned)
        high = weighted.astype(BF)
        low = (weighted - high.astype(F32)).astype(BF)
        row_sum = nn(high, tcol[...]) + nn(low, tcol[...])
        keep = spread(mirrored).astype(BF)
        col_sum = tn(high * keep, row_wide[:, NB:]) + tn(low * keep, row_wide[:, NB:])
        col_out[...] += col_sum.reshape(col_out.shape)
        row_out[2 * t : 2 * t + 2] = row_sum.reshape(2, 2 * FB, NT)


def tile_call(me, rows, packed, tcol, kern, owned, mirrored, col_in=None):
    vmem = pl.BlockSpec(memory_space=pltpu.VMEM)
    hbm = pl.BlockSpec(memory_space=pltpu.HBM)
    in_specs = [pl.BlockSpec(memory_space=pltpu.SMEM), hbm, hbm, vmem, hbm, vmem, vmem]
    args = [me, rows, packed, tcol, kern, owned, mirrored]
    if col_in is not None:
        in_specs.append(vmem)
        args.append(col_in)
    return pl.pallas_call(
        tile_kernel,
        in_specs=in_specs,
        out_specs=[vmem] * 2,
        out_shape=[jax.ShapeDtypeStruct((4, 2 * FB, NT), F32), jax.ShapeDtypeStruct((N_ROW, FB, NT), F32)],
        scratch_shapes=[
            pltpu.VMEM((NB, POINTS), BF),
            pltpu.VMEM((2, 4, FB, WIDE), BF),
            pltpu.VMEM((2, 4, FB * COL_PTS // 128, 128), F32),
            pltpu.SemaphoreType.DMA((17,)),
        ],
        compiler_params=pltpu.CompilerParams(vmem_limit_bytes=52 * 2**20),
        cost_estimate=pl.CostEstimate(flops=5_000_000_000, bytes_accessed=13_000_000, transcendentals=0),
        name="own_core_tiles" if col_in is not None else "other_core_tiles",
    )(*args)


def local(orbitals, targets, kernel, tile_owner):
    r, c = lax.axis_index("row"), lax.axis_index("col")
    z, xl, k = c // 4, c // 2 % 2, c % 2

    packed = pack(orbitals, targets).reshape(DEVICES, 8, SENT)
    packed = lax.all_to_all(packed, AXES, split_axis=0, concat_axis=0, tiled=True)
    packed = packed.reshape(DEVICES * 8, SENT)
    rows_other, tcol = unpack(packed)
    rows_own = send(rows_other, k=1)

    flags = tile_owner.reshape(N_COL, N_ROW).astype(F32)
    here = (lax.broadcasted_iota(jnp.int32, flags.shape, 0) == c) & (
        lax.broadcasted_iota(jnp.int32, flags.shape, 1) == r
    )
    owned = jnp.repeat(flags, FB, axis=1).reshape(4, 2, 2, 1, COL_PTS)
    mirrored = jnp.repeat(jnp.where(here, 0.0, flags), FB, axis=1).reshape(4, 2, 2, 1, COL_PTS)
    kern = kernel.reshape(4, 2, 2, FB * COL_PTS // 128, 128)

    def me(core):
        return jnp.stack([z, xl, core]).astype(jnp.int32)

    row_other, col_part = tile_call(me(1 - k), rows_other, packed, tcol, kern, owned, mirrored)
    row_own, col_sum = tile_call(me(k), rows_own, packed, tcol, kern, owned, mirrored, col_part)

    row_sum = row_own + send(row_other, k=1)
    row_sum = row_sum[0] + send(row_sum[1], z=1) + send(row_sum[2], z=2) + send(row_sum[3], z=3)
    row_share = row_sum[:FB] + send(row_sum[FB:], xl=1)
    col_share = lax.all_to_all(col_sum, "row", split_axis=0, concat_axis=0, tiled=True).sum(axis=0)
    return row_share + col_share


def solution(mesh):
    in_specs = (
        P(("row", "col"), None),
        P(("row", "col"), None),
        P("row", "col", None),
        P("row", None, None, "col"),
    )
    out_specs = P(("row", "col"), None)
    return jax.shard_map(local, mesh=mesh, in_specs=in_specs, out_specs=out_specs, check_vma=False)
```

```python
import functools
import itertools

import jax
import jax.numpy as jnp
from jax import lax
from jax.experimental import pallas as pl
from jax.experimental.pallas import tpu as pltpu
from jax.sharding import PartitionSpec as P

N_ROW, N_COL, FB, NB, NT = 8, 16, 160, 1024, 128
DEVICES = N_ROW * N_COL
ROW_PTS, COL_PTS = N_COL * FB, N_ROW * FB
WIDE = NB + NT
AXES = ("row", "col")
PARTS = {"y": 4, "xh": 2, "z": 4, "xl": 2, "k": 2}
TILE = 4 * FB
BF, F32 = jnp.bfloat16, jnp.float32


def index_of(y, xh, z, xl, k):
    return (y * 2 + xh) * N_COL + z * 4 + xl * 2 + k


def moved(**steps):
    pairs = []
    for at in itertools.product(*map(range, PARTS.values())):
        to = [(a + steps.get(name, 0)) % size for a, (name, size) in zip(at, PARTS.items())]
        pairs.append((index_of(*at), index_of(*to)))
    return pairs


def send(x, **steps):
    return lax.ppermute(x, AXES, moved(**steps))


def nn(a, b):
    return jnp.dot(a, b, preferred_element_type=F32)


def nt(a, b):
    return lax.dot_general(a, b, (((1,), (1,)), ((), ())), preferred_element_type=F32)


def tn(a, b):
    return lax.dot_general(a, b, (((0,), (0,)), ((), ())), preferred_element_type=F32)


def points(ref, block):
    return ref[:, block * FB : (block + 1) * FB].astype(F32)


def pack_kernel(orb, tgt, out):
    row = lax.broadcasted_iota(jnp.int32, (8, FB), 0)
    for pair in range(DEVICES // 2):
        blocks = []
        for q in (2 * pair, 2 * pair + 1):
            sources = (q, q ^ 16, q ^ 2)
            extra = jnp.where(
                row == 0,
                points(tgt, sources[0]),
                jnp.where(row == 1, points(tgt, sources[1]), points(tgt, sources[2])),
            )
            pieces = [points(orb, s) for s in sources]
            blocks.append(jnp.concatenate([*pieces, extra], axis=1))
        out[16 * pair : 16 * (pair + 1), :] = jnp.concatenate(blocks, axis=0).astype(BF)


def pack(orbitals, targets):
    return pl.pallas_call(
        pack_kernel,
        out_shape=jax.ShapeDtypeStruct((DEVICES * 8, 4 * FB), BF),
        compiler_params=pltpu.CompilerParams(vmem_limit_bytes=32 * 2**20),
        name="pack",
    )(orbitals, targets)


def unpack_kernel(packed, cols, rows):
    turned = packed[:, : 3 * FB].T
    cols[: FB, :NB] = turned[:FB]
    cols[FB:, :NB] = turned[FB : 2 * FB]
    rows[:FB, :NB] = turned[:FB]
    rows[FB:, :NB] = turned[2 * FB :]
    source = lax.broadcasted_iota(jnp.int32, (NB, NT), 0)
    target = lax.broadcasted_iota(jnp.int32, (NB, NT), 1)
    mine, col_side, row_side = (
        tn(packed[...], jnp.where(source == 8 * target + i, 1.0, 0.0).astype(BF))[3 * FB :].astype(BF) for i in range(3)
    )
    cols[:FB, NB:] = mine
    cols[FB:, NB:] = col_side
    rows[:FB, NB:] = mine
    rows[FB:, NB:] = row_side


def unpack(packed):
    return pl.pallas_call(
        unpack_kernel,
        out_shape=[jax.ShapeDtypeStruct((2 * FB, WIDE), BF)] * 2,
        compiler_params=pltpu.CompilerParams(vmem_limit_bytes=32 * 2**20),
        name="unpack",
    )(packed)


def tile_kernel(z_steps, me, *refs):
    tiles = len(z_steps)
    far = tiles == 1
    n_rows = 2 * tiles
    row_refs, refs = refs[:n_rows], refs[n_rows:]
    (pair, down, up, far_own, far_other, kern, owned, mirrored), refs = refs[:8], refs[8:]
    if far:
        col_in, refs = refs[0], refs[1:]
    row_own, row_other, col_out, cols, rows, stored, sems = refs
    y, xh, z, xl, k = (me[i] for i in range(5))

    def block(y_step, side):
        return lax.rem(y + y_step, 4) * 2 + lax.rem(xh + side, 2)

    count = [0]

    def start(src, dst):
        copy = pltpu.make_async_copy(src, dst, sems.at[count[0]])
        count[0] += 1
        copy.start()
        return copy

    def tile_copies(t):
        z_at = lax.rem(z + z_steps[t], 4)
        found = []
        found += [start(row_refs[2 * t + b], rows.at[t, pl.ds(2 * b, 2)]) for b in range(2)]
        for b in range(4):
            found.append(start(kern.at[z_at, lax.rem(xl + b % 2, 2), lax.rem(k + b // 2, 2)], stored.at[t, b]))
        return found

    pieces = [(ref.at[side], block(step, side)) for ref, step in ((pair, 0), (down, 3), (up, 1)) for side in (0, 1)]
    pieces += [(far_own, block(2, 0)), (far_other, block(2, 1))]
    col_copies = [start(src, cols.at[at]) for src, at in pieces]
    row_copies = [tile_copies(t) for t in range(tiles)]
    if far:
        col_out[...] = col_in[...]
    else:
        col_out[...] = jnp.zeros_like(col_out)
    for copy in col_copies:
        copy.wait()
    col_wide = cols[...].reshape(COL_PTS, WIDE)

    for t in range(tiles):
        z_at = lax.rem(z + z_steps[t], 4)
        for copy in row_copies[t]:
            copy.wait()
        row_wide = rows[t].reshape(TILE, WIDE)
        gram = nt(row_wide[:, :NB], col_wide[:, :NB])
        chunks = COL_PTS // 128
        values = jnp.concatenate(
            [
                jnp.concatenate([stored[t, b, pl.ds(j, FB, stride=chunks), :] for j in range(chunks)], axis=1)
                for b in range(4)
            ],
            axis=0,
        )

        def spread(ref):
            return jnp.concatenate(
                [
                    jnp.broadcast_to(ref[z_at, lax.rem(xl + b % 2, 2), lax.rem(k + b // 2, 2)], (FB, COL_PTS))
                    for b in range(4)
                ],
                axis=0,
            )

        weighted = gram * values * spread(owned)
        high = weighted.astype(BF)
        low = (weighted - high.astype(F32)).astype(BF)
        row_sum = nn(high, col_wide[:, NB:]) + nn(low, col_wide[:, NB:])
        keep = spread(mirrored).astype(BF)
        col_sum = tn(high * keep, row_wide[:, NB:]) + tn(low * keep, row_wide[:, NB:])
        col_out[...] += col_sum.reshape(col_out.shape)
        row_own[t] = row_sum[: 2 * FB]
        row_other[t] = row_sum[2 * FB :]


def tile_call(z_steps, me, rows, col_parts, kern, owned, mirrored, col_in=None):
    tiles = len(z_steps)
    vmem = pl.BlockSpec(memory_space=pltpu.VMEM)
    hbm = pl.BlockSpec(memory_space=pltpu.HBM)
    in_specs = [pl.BlockSpec(memory_space=pltpu.SMEM)] + [hbm] * (len(rows) + len(col_parts) + 1) + [vmem] * 2
    args = [me, *rows, *col_parts, kern, owned, mirrored]
    if col_in is not None:
        in_specs.append(vmem)
        args.append(col_in)
    copies = 8 + len(rows) + 4 * tiles
    return pl.pallas_call(
        functools.partial(tile_kernel, z_steps),
        in_specs=in_specs,
        out_specs=[vmem] * 3,
        out_shape=[jax.ShapeDtypeStruct((tiles, 2 * FB, NT), F32)] * 2 + [jax.ShapeDtypeStruct((N_ROW, FB, NT), F32)],
        scratch_shapes=[
            pltpu.VMEM((N_ROW, FB, WIDE), BF),
            pltpu.VMEM((tiles, 4, FB, WIDE), BF),
            pltpu.VMEM((tiles, 4, FB * COL_PTS // 128, 128), F32),
            pltpu.SemaphoreType.DMA((copies,)),
        ],
        compiler_params=pltpu.CompilerParams(vmem_limit_bytes=52 * 2**20),
        cost_estimate=pl.CostEstimate(
            flops=2_600_000_000 * tiles, bytes_accessed=5_000_000 * tiles, transcendentals=0
        ),
        name="near_tiles" if tiles > 1 else "far_tile",
    )(*args)


def halves(pair):
    return pair.reshape(2, FB, pair.shape[-1])


def local(orbitals, targets, kernel, tile_owner):
    r, c = lax.axis_index("row"), lax.axis_index("col")
    me = jnp.stack([r // 2, r % 2, c // 4, c // 2 % 2, c % 2]).astype(jnp.int32)

    packed = pack(orbitals, targets).reshape(DEVICES, 8, 4 * FB)
    packed = lax.all_to_all(packed, AXES, split_axis=0, concat_axis=0, tiled=True)
    pair_y, pair_z = unpack(packed.reshape(DEVICES * 8, 4 * FB))

    y_down, y_up = send(pair_y, y=1), send(pair_y, y=3)
    z_down, z_up = send(pair_z, z=1), send(pair_z, z=3)
    y_far, y_far_other = send(y_down[:FB], y=1), send(y_up[FB:], y=3)
    col_parts = (halves(pair_y), halves(y_down), halves(y_up), y_far, y_far_other)
    across = [send(own, k=1) for own in (pair_z, z_up, z_down)]
    near_rows = [halves(part) for both in zip((pair_z, z_up, z_down), across) for part in both]
    far_rows = [halves(send(z_down, z=1)), halves(send(across[1], z=3))]

    flags = tile_owner.reshape(N_COL, N_ROW).astype(F32)
    here = (lax.broadcasted_iota(jnp.int32, flags.shape, 0) == c) & (
        lax.broadcasted_iota(jnp.int32, flags.shape, 1) == r
    )
    owned = jnp.repeat(flags, FB, axis=1).reshape(4, 2, 2, 1, COL_PTS)
    mirrored = jnp.repeat(jnp.where(here, 0.0, flags), FB, axis=1).reshape(4, 2, 2, 1, COL_PTS)
    kern = kernel.reshape(4, 2, 2, FB * COL_PTS // 128, 128)

    near_own, near_other, col_part = tile_call((0, 1, 3), me, near_rows, col_parts, kern, owned, mirrored)
    far_own, far_other, col_sum = tile_call((2,), me, far_rows, col_parts, kern, owned, mirrored, col_part)

    near = near_own + send(near_other, k=1)
    far = send(far_own[0], z=2) + send(far_other[0], z=2, k=1)
    row_sum = near[0] + send(near[1], z=1) + send(near[2], z=3) + far
    row_share = row_sum[:FB] + send(row_sum[FB:], xl=1)
    col_share = lax.all_to_all(col_sum, "row", split_axis=0, concat_axis=0, tiled=True).sum(axis=0)
    return row_share + col_share


def solution(mesh):
    in_specs = (
        P(("row", "col"), None),
        P(("row", "col"), None),
        P("row", "col", None),
        P("row", None, None, "col"),
    )
    out_specs = P(("row", "col"), None)
    return jax.shard_map(local, mesh=mesh, in_specs=in_specs, out_specs=out_specs, check_vma=False)
```

```python
import functools
import itertools

import jax
import jax.numpy as jnp
from jax import lax
from jax.experimental import pallas as pl
from jax.experimental.pallas import tpu as pltpu
from jax.sharding import PartitionSpec as P

N_ROW, N_COL, FB, NB, NT = 8, 16, 160, 1024, 128
DEVICES = N_ROW * N_COL
ROW_PTS, COL_PTS = N_COL * FB, N_ROW * FB
WIDE = NB + NT
AXES = ("row", "col")
PARTS = {"y": 4, "xh": 2, "z": 4, "xl": 2, "k": 2}
TILE = 4 * FB
BF, F32 = jnp.bfloat16, jnp.float32


def index_of(y, xh, z, xl, k):
    return (y * 2 + xh) * N_COL + z * 4 + xl * 2 + k


def moved(**steps):
    pairs = []
    for at in itertools.product(*map(range, PARTS.values())):
        to = [(a + steps.get(name, 0)) % size for a, (name, size) in zip(at, PARTS.items())]
        pairs.append((index_of(*at), index_of(*to)))
    return pairs


def send(x, **steps):
    return lax.ppermute(x, AXES, moved(**steps))


def nn(a, b):
    return jnp.dot(a, b, preferred_element_type=F32)


def nt(a, b):
    return lax.dot_general(a, b, (((1,), (1,)), ((), ())), preferred_element_type=F32)


def tn(a, b):
    return lax.dot_general(a, b, (((0,), (0,)), ((), ())), preferred_element_type=F32)


def points(ref, block):
    return ref[:, block * FB : (block + 1) * FB].astype(F32)


def pack_kernel(orb, tgt, out):
    row = lax.broadcasted_iota(jnp.int32, (8, FB), 0)
    for pair in range(DEVICES // 2):
        blocks = []
        for q in (2 * pair, 2 * pair + 1):
            sources = (q, q ^ 16, q ^ 2)
            extra = jnp.where(
                row == 0,
                tgt[sources[0] : sources[0] + 1, :],
                jnp.where(row == 1, tgt[sources[1] : sources[1] + 1, :], tgt[sources[2] : sources[2] + 1, :]),
            )
            pieces = [points(orb, s) for s in sources]
            blocks.append(jnp.concatenate([*pieces, extra], axis=1))
        out[16 * pair : 16 * (pair + 1), :] = jnp.concatenate(blocks, axis=0).astype(BF)


def pack(orbitals, targets):
    return pl.pallas_call(
        pack_kernel,
        out_shape=jax.ShapeDtypeStruct((DEVICES * 8, 4 * FB), BF),
        compiler_params=pltpu.CompilerParams(vmem_limit_bytes=32 * 2**20),
        name="pack",
    )(orbitals, targets.astype(F32).reshape(DEVICES, FB))


def unpack_kernel(packed, own, beside, rows):
    turned = packed[:, : 3 * FB].T
    own[:, :NB] = turned[:FB]
    beside[:, :NB] = turned[FB : 2 * FB]
    rows[:FB, :NB] = turned[:FB]
    rows[FB:, :NB] = turned[2 * FB :]
    source = lax.broadcasted_iota(jnp.int32, (NB, NT), 0)
    target = lax.broadcasted_iota(jnp.int32, (NB, NT), 1)
    mine, col_side, row_side = (
        tn(packed[...], jnp.where(source == 8 * target + i, 1.0, 0.0).astype(BF))[3 * FB :].astype(BF) for i in range(3)
    )
    own[:, NB:] = mine
    beside[:, NB:] = col_side
    rows[:FB, NB:] = mine
    rows[FB:, NB:] = row_side


def unpack(packed):
    return pl.pallas_call(
        unpack_kernel,
        out_shape=[jax.ShapeDtypeStruct((n * FB, WIDE), BF) for n in (1, 1, 2)],
        compiler_params=pltpu.CompilerParams(vmem_limit_bytes=32 * 2**20),
        name="unpack",
    )(packed)


def tile_kernel(z_steps, me, *refs):
    tiles = len(z_steps)
    far = tiles == 1
    n_rows = 2 * tiles
    row_refs, refs = refs[:n_rows], refs[n_rows:]
    col_refs, (kern, owned, mirrored), refs = refs[:8], refs[8:11], refs[11:]
    if far:
        col_in, refs = refs[0], refs[1:]
    row_own, row_other, *col_outs, cols, rows, stored, col_sum, sems = refs
    y, xh, z, xl, k = (me[i] for i in range(5))

    def block(y_step, side):
        return lax.rem(y + y_step, 4) * 2 + lax.rem(xh + side, 2)

    count = [0]

    def start(src, dst):
        copy = pltpu.make_async_copy(src, dst, sems.at[count[0]])
        count[0] += 1
        copy.start()
        return copy

    def row_copies(t):
        return [start(row_refs[2 * t + b], rows.at[t, pl.ds(2 * b, 2)]) for b in range(2)]

    def kern_copies(t):
        z_at = lax.rem(z + z_steps[t], 4)
        return [
            start(kern.at[z_at, lax.rem(xl + b % 2, 2), lax.rem(k + b // 2, 2)], stored.at[t, b]) for b in range(4)
        ]

    pieces = [(ref, block(i // 2, i % 2)) for i, ref in enumerate(col_refs)]
    first_copies = [start(src, cols.at[at]) for src, at in pieces] + row_copies(0)
    next_rows, next_kern = [], kern_copies(0)
    if far:
        col_sum[...] = col_in[...]
    else:
        col_sum[...] = jnp.zeros_like(col_sum)
    for copy in first_copies:
        copy.wait()
    col_wide = cols[...].reshape(COL_PTS, WIDE)

    for t in range(tiles):
        z_at = lax.rem(z + z_steps[t], 4)
        for copy in next_rows:
            copy.wait()
        kern_here = next_kern
        if t + 1 < tiles:
            next_rows, next_kern = row_copies(t + 1), kern_copies(t + 1)
        row_wide = rows[t].reshape(TILE, WIDE)
        gram = nt(row_wide[:, :NB], col_wide[:, :NB])
        for copy in kern_here:
            copy.wait()
        chunks = COL_PTS // 128
        values = jnp.concatenate(
            [
                jnp.concatenate([stored[t, b, pl.ds(j, FB, stride=chunks), :] for j in range(chunks)], axis=1)
                for b in range(4)
            ],
            axis=0,
        )

        def spread(ref):
            return jnp.concatenate(
                [
                    jnp.broadcast_to(ref[z_at, lax.rem(xl + b % 2, 2), lax.rem(k + b // 2, 2)], (FB, COL_PTS))
                    for b in range(4)
                ],
                axis=0,
            )

        weighted = gram * values * spread(owned)
        high = weighted.astype(BF)
        low = (weighted - high.astype(F32)).astype(BF)
        row_sum = nn(high, col_wide[:, NB:]) + nn(low, col_wide[:, NB:])
        keep = spread(mirrored).astype(BF)
        added = tn(high * keep, row_wide[:, NB:]) + tn(low * keep, row_wide[:, NB:])
        col_sum[...] += added.reshape(col_sum.shape)
        row_own[t] = row_sum[: 2 * FB]
        row_other[t] = row_sum[2 * FB :]

    if not far:
        col_outs[0][...] = col_sum[...]
    else:
        for step, col_out in enumerate(col_outs):
            for side in (0, 1):
                col_out[side * FB : (side + 1) * FB, :] = col_sum[block(step, side)]


def tile_call(z_steps, me, rows, col_parts, kern, owned, mirrored, col_in=None):
    tiles = len(z_steps)
    vmem = pl.BlockSpec(memory_space=pltpu.VMEM)
    hbm = pl.BlockSpec(memory_space=pltpu.HBM)
    in_specs = [pl.BlockSpec(memory_space=pltpu.SMEM)] + [hbm] * (len(rows) + len(col_parts) + 1) + [vmem] * 2
    args = [me, *rows, *col_parts, kern, owned, mirrored]
    if col_in is not None:
        in_specs.append(vmem)
        args.append(col_in)
    copies = 8 + len(rows) + 4 * tiles
    if col_in is None:
        col_shapes = [jax.ShapeDtypeStruct((N_ROW, FB, NT), F32)]
    else:
        col_shapes = [jax.ShapeDtypeStruct((2 * FB, NT), F32)] * 4
    return pl.pallas_call(
        functools.partial(tile_kernel, z_steps),
        in_specs=in_specs,
        out_specs=[vmem] * (2 + len(col_shapes)),
        out_shape=[jax.ShapeDtypeStruct((tiles, 2 * FB, NT), F32)] * 2 + col_shapes,
        scratch_shapes=[
            pltpu.VMEM((N_ROW, FB, WIDE), BF),
            pltpu.VMEM((tiles, 4, FB, WIDE), BF),
            pltpu.VMEM((tiles, 4, FB * COL_PTS // 128, 128), F32),
            pltpu.VMEM((N_ROW, FB, NT), F32),
            pltpu.SemaphoreType.DMA((copies,)),
        ],
        compiler_params=pltpu.CompilerParams(vmem_limit_bytes=(46 if tiles > 1 else 52) * 2**20),
        cost_estimate=pl.CostEstimate(
            flops=2_600_000_000 * tiles, bytes_accessed=5_000_000 * tiles, transcendentals=0
        ),
        name="near_tiles" if tiles > 1 else "far_tile",
    )(*args)


def halves(pair):
    return pair.reshape(2, FB, pair.shape[-1])


def local(orbitals, targets, kernel, tile_owner):
    r, c = lax.axis_index("row"), lax.axis_index("col")
    me = jnp.stack([r // 2, r % 2, c // 4, c // 2 % 2, c % 2]).astype(jnp.int32)

    packed = pack(orbitals, targets).reshape(DEVICES, 8, 4 * FB)
    packed = lax.all_to_all(packed, AXES, split_axis=0, concat_axis=0, tiled=True)
    own, beside, pair_z = unpack(packed.reshape(DEVICES * 8, 4 * FB))

    own_down, beside_up = send(own, y=1), send(beside, y=3)
    z_down, z_up = send(pair_z, z=1), send(pair_z, z=3)
    beside_down, own_up = send(beside, y=1), send(own, y=3)
    own_far, beside_far = send(own_down, y=1), send(beside_up, y=3)
    col_parts = (own, beside, own_up, beside_up, own_far, beside_far, own_down, beside_down)
    across = [send(own, k=1) for own in (pair_z, z_up, z_down)]
    near_rows = [halves(part) for both in zip((pair_z, z_up, z_down), across) for part in both]
    far_rows = [halves(send(z_down, z=1)), halves(send(across[1], z=3))]

    flags = tile_owner.reshape(N_COL, N_ROW).astype(F32)
    here = (lax.broadcasted_iota(jnp.int32, flags.shape, 0) == c) & (
        lax.broadcasted_iota(jnp.int32, flags.shape, 1) == r
    )
    owned = jnp.repeat(flags, FB, axis=1).reshape(4, 2, 2, 1, COL_PTS)
    mirrored = jnp.repeat(jnp.where(here, 0.0, flags), FB, axis=1).reshape(4, 2, 2, 1, COL_PTS)
    kern = kernel.reshape(4, 2, 2, FB * COL_PTS // 128, 128)

    near_own, near_other, col_part = tile_call((0, 1, 3), me, near_rows, col_parts, kern, owned, mirrored)
    near = near_own + send(near_other, k=1)
    near, col_part = lax.optimization_barrier((near, col_part))
    row_up, row_down = send(near[1], z=1), send(near[2], z=3)
    far_own, far_other, c0, c1, c2, c3 = tile_call((2,), me, far_rows, col_parts, kern, owned, mirrored, col_part)

    row_sum = near[0] + row_up + row_down + send(far_own[0], z=2) + send(far_other[0], z=2, k=1)
    col_sum = c0 + send(c1, y=1) + send(c2, y=2) + send(c3, y=3)
    row_share = row_sum[:FB] + send(row_sum[FB:], xl=1)
    col_share = col_sum[:FB] + send(col_sum[FB:], xh=1)
    return row_share + col_share


def solution(mesh):
    in_specs = (
        P(("row", "col"), None),
        P(("row", "col"), None),
        P("row", "col", None),
        P("row", None, None, "col"),
    )
    out_specs = P(("row", "col"), None)
    return jax.shard_map(local, mesh=mesh, in_specs=in_specs, out_specs=out_specs, check_vma=False)
```

```python
import itertools

import jax
import jax.numpy as jnp
from jax import lax
from jax.experimental import pallas as pl
from jax.experimental.pallas import tpu as pltpu
from jax.sharding import PartitionSpec as P

N_ROW, N_COL, FB, NB, NT = 8, 16, 160, 1024, 128
DEVICES = N_ROW * N_COL
ROW_PTS, COL_PTS = N_COL * FB, N_ROW * FB
WIDE = NB + NT
AXES = ("row", "col")
PARTS = {"y": 4, "xh": 2, "z": 4, "xl": 2, "k": 2}
TILE = 4 * FB
BF, F32 = jnp.bfloat16, jnp.float32


def index_of(y, xh, z, xl, k):
    return (y * 2 + xh) * N_COL + z * 4 + xl * 2 + k


def moved(**steps):
    pairs = []
    for at in itertools.product(*map(range, PARTS.values())):
        to = [(a + steps.get(name, 0)) % size for a, (name, size) in zip(at, PARTS.items())]
        pairs.append((index_of(*at), index_of(*to)))
    return pairs


def send(x, **steps):
    return lax.ppermute(x, AXES, moved(**steps))


def nn(a, b):
    return jnp.dot(a, b, preferred_element_type=F32)


def nt(a, b):
    return lax.dot_general(a, b, (((1,), (1,)), ((), ())), preferred_element_type=F32)


def tn(a, b):
    return lax.dot_general(a, b, (((0,), (0,)), ((), ())), preferred_element_type=F32)


def points(ref, block):
    return ref[:, block * FB : (block + 1) * FB].astype(F32)


def pack_kernel(orb, tgt, out):
    row = lax.broadcasted_iota(jnp.int32, (8, FB), 0)
    for pair in range(DEVICES // 2):
        blocks = []
        for q in (2 * pair, 2 * pair + 1):
            sources = (q, q ^ 16, q ^ 2)
            extra = jnp.where(
                row == 0,
                tgt[sources[0] : sources[0] + 1, :],
                jnp.where(row == 1, tgt[sources[1] : sources[1] + 1, :], tgt[sources[2] : sources[2] + 1, :]),
            )
            pieces = [points(orb, s) for s in sources]
            blocks.append(jnp.concatenate([*pieces, extra], axis=1))
        out[16 * pair : 16 * (pair + 1), :] = jnp.concatenate(blocks, axis=0).astype(BF)


def pack(orbitals, targets):
    return pl.pallas_call(
        pack_kernel,
        out_shape=jax.ShapeDtypeStruct((DEVICES * 8, 4 * FB), BF),
        compiler_params=pltpu.CompilerParams(vmem_limit_bytes=32 * 2**20),
        name="pack",
    )(orbitals, targets.astype(F32).reshape(DEVICES, FB))


def unpack_kernel(packed, own, col_side, row_side):
    turned = packed[:, : 3 * FB].T
    source = lax.broadcasted_iota(jnp.int32, (NB, NT), 0)
    target = lax.broadcasted_iota(jnp.int32, (NB, NT), 1)
    for i, out in enumerate((own, col_side, row_side)):
        out[:, :NB] = turned[i * FB : (i + 1) * FB]
        chosen = jnp.where(source == 8 * target + i, 1.0, 0.0).astype(BF)
        out[:, NB:] = tn(packed[:, 3 * FB :], chosen).astype(BF)


def unpack(packed):
    return pl.pallas_call(
        unpack_kernel,
        out_shape=[jax.ShapeDtypeStruct((FB, WIDE), BF)] * 3,
        compiler_params=pltpu.CompilerParams(vmem_limit_bytes=32 * 2**20),
        name="unpack",
    )(packed)


def tile_kernel(me, *refs):
    row_refs, col_refs, (kern, owned, mirrored), refs = refs[:16], refs[16:24], refs[24:27], refs[27:]
    row_own, row_other, c0, c1, c2, c3, cols, rows, stored, col_sum, sems = refs
    y, xh, z, xl, k = (me[i] for i in range(5))
    count = [0]

    def start(src, dst):
        copy = pltpu.make_async_copy(src, dst, sems.at[count[0]])
        count[0] += 1
        copy.start()
        return copy

    def block(y_step, side):
        return lax.rem(y + y_step, 4) * 2 + lax.rem(xh + side, 2)

    def place(t, b):
        return lax.rem(z + t, 4), lax.rem(xl + b % 2, 2), lax.rem(k + b // 2, 2)

    def row_copies(t):
        return [start(row_refs[4 * t + b], rows.at[t, b]) for b in range(4)]

    def kern_copies(t):
        return [start(kern.at[place(t, b)], stored.at[t % 2, b]) for b in range(4)]

    first_copies = [start(ref, cols.at[block(i // 2, i % 2)]) for i, ref in enumerate(col_refs)] + row_copies(0)
    next_rows, next_kern = [], kern_copies(0)
    col_sum[...] = jnp.zeros_like(col_sum)
    for copy in first_copies:
        copy.wait()
    col_wide = cols[...].reshape(COL_PTS, WIDE)

    for t in range(4):
        for copy in next_rows:
            copy.wait()
        kern_here = next_kern
        if t < 3:
            next_rows, next_kern = row_copies(t + 1), kern_copies(t + 1)
        row_wide = rows[t].reshape(TILE, WIDE)
        gram = nt(row_wide[:, :NB], col_wide[:, :NB])
        for copy in kern_here:
            copy.wait()
        chunks = COL_PTS // 128
        values = jnp.concatenate(
            [
                jnp.concatenate([stored[t % 2, b, pl.ds(j, FB, stride=chunks), :] for j in range(chunks)], axis=1)
                for b in range(4)
            ],
            axis=0,
        )

        def spread(ref):
            return jnp.concatenate([jnp.broadcast_to(ref[place(t, b)], (FB, COL_PTS)) for b in range(4)], axis=0)

        weighted = gram * values * spread(owned)
        high = weighted.astype(BF)
        low = (weighted - high.astype(F32)).astype(BF)
        row_sum = nn(high, col_wide[:, NB:]) + nn(low, col_wide[:, NB:])
        keep = spread(mirrored).astype(BF)
        added = tn(high * keep, row_wide[:, NB:]) + tn(low * keep, row_wide[:, NB:])
        col_sum[...] += added.reshape(col_sum.shape)
        row_own[t] = row_sum[: 2 * FB]
        row_other[t] = row_sum[2 * FB :]

    for step, col_out in enumerate((c0, c1, c2, c3)):
        for side in (0, 1):
            col_out[side * FB : (side + 1) * FB, :] = col_sum[block(step, side)]


def tile_call(me, row_parts, col_parts, kern, owned, mirrored):
    vmem = pl.BlockSpec(memory_space=pltpu.VMEM)
    hbm = pl.BlockSpec(memory_space=pltpu.HBM)
    return pl.pallas_call(
        tile_kernel,
        in_specs=[pl.BlockSpec(memory_space=pltpu.SMEM)] + [hbm] * 25 + [vmem] * 2,
        out_specs=[vmem] * 6,
        out_shape=[jax.ShapeDtypeStruct((4, 2 * FB, NT), F32)] * 2 + [jax.ShapeDtypeStruct((2 * FB, NT), F32)] * 4,
        scratch_shapes=[
            pltpu.VMEM((N_ROW, FB, WIDE), BF),
            pltpu.VMEM((4, 4, FB, WIDE), BF),
            pltpu.VMEM((2, 4, FB * COL_PTS // 128, 128), F32),
            pltpu.VMEM((N_ROW, FB, NT), F32),
            pltpu.SemaphoreType.DMA((40,)),
        ],
        compiler_params=pltpu.CompilerParams(vmem_limit_bytes=52 * 2**20),
        cost_estimate=pl.CostEstimate(flops=10_000_000_000, bytes_accessed=24_000_000, transcendentals=0),
        name="tiles",
    )(me, *row_parts, *col_parts, kern, owned, mirrored)


def ring(block, beside, axis):
    down, beside_up = send(block, **{axis: 1}), send(beside, **{axis: 3})
    beside_down, up = send(beside, **{axis: 1}), send(block, **{axis: 3})
    far, beside_far = send(down, **{axis: 1}), send(beside_up, **{axis: 3})
    return (block, beside, up, beside_up, far, beside_far, down, beside_down)


def local(orbitals, targets, kernel, tile_owner):
    r, c = lax.axis_index("row"), lax.axis_index("col")
    me = jnp.stack([r // 2, r % 2, c // 4, c // 2 % 2, c % 2]).astype(jnp.int32)

    packed = pack(orbitals, targets).reshape(DEVICES, 8, 4 * FB)
    packed = lax.all_to_all(packed, AXES, split_axis=0, concat_axis=0, tiled=True)
    own, col_side, row_side = unpack(packed.reshape(DEVICES * 8, 4 * FB))
    col_parts = ring(own, col_side, "y")
    same = ring(own, row_side, "z")
    other = [send(block, k=1) for block in same]
    row_parts = [block for t in range(0, 8, 2) for block in (*same[t : t + 2], *other[t : t + 2])]

    flags = tile_owner.reshape(N_COL, N_ROW).astype(F32)
    here = (lax.broadcasted_iota(jnp.int32, flags.shape, 0) == c) & (
        lax.broadcasted_iota(jnp.int32, flags.shape, 1) == r
    )
    owned = jnp.repeat(flags, FB, axis=1).reshape(4, 2, 2, 1, COL_PTS)
    mirrored = jnp.repeat(jnp.where(here, 0.0, flags), FB, axis=1).reshape(4, 2, 2, 1, COL_PTS)
    kern = kernel.reshape(4, 2, 2, FB * COL_PTS // 128, 128)

    row_own, row_other, c0, c1, c2, c3 = tile_call(me, row_parts, col_parts, kern, owned, mirrored)

    col_sum = c0 + send(c2, y=2) + send(c1, y=1) + send(c3, y=3)
    row_sum = row_own + send(row_other, k=1)
    row_sum = row_sum[0] + send(row_sum[2], z=2) + send(row_sum[1], z=1) + send(row_sum[3], z=3)
    row_share = row_sum[:FB] + send(row_sum[FB:], xl=1)
    col_share = col_sum[:FB] + send(col_sum[FB:], xh=1)
    return row_share + col_share


def solution(mesh):
    in_specs = (
        P(("row", "col"), None),
        P(("row", "col"), None),
        P("row", "col", None),
        P("row", None, None, "col"),
    )
    out_specs = P(("row", "col"), None)
    return jax.shard_map(local, mesh=mesh, in_specs=in_specs, out_specs=out_specs, check_vma=False)
```

```python
import itertools

import jax
import jax.numpy as jnp
from jax import lax
from jax.experimental import pallas as pl
from jax.experimental.pallas import tpu as pltpu
from jax.sharding import PartitionSpec as P

N_ROW, N_COL, FB, NB, NT = 8, 16, 160, 1024, 128
DEVICES = N_ROW * N_COL
ROW_PTS, COL_PTS = N_COL * FB, N_ROW * FB
WIDE = NB + NT
AXES = ("row", "col")
PARTS = {"y": 4, "xh": 2, "z": 4, "xl": 2, "k": 2}
TILE = 4 * FB
BF, F32 = jnp.bfloat16, jnp.float32


def index_of(y, xh, z, xl, k):
    return (y * 2 + xh) * N_COL + z * 4 + xl * 2 + k


def moved(**steps):
    pairs = []
    for at in itertools.product(*map(range, PARTS.values())):
        to = [(a + steps.get(name, 0)) % size for a, (name, size) in zip(at, PARTS.items())]
        pairs.append((index_of(*at), index_of(*to)))
    return pairs


def send(x, **steps):
    return lax.ppermute(x, AXES, moved(**steps))


def nn(a, b):
    return jnp.dot(a, b, preferred_element_type=F32)


def nt(a, b):
    return lax.dot_general(a, b, (((1,), (1,)), ((), ())), preferred_element_type=F32)


def tn(a, b):
    return lax.dot_general(a, b, (((0,), (0,)), ((), ())), preferred_element_type=F32)


def points(ref, block):
    return ref[:, block * FB : (block + 1) * FB].astype(F32)


def pack_kernel(orb, tgt, out):
    row = lax.broadcasted_iota(jnp.int32, (8, FB), 0)
    for pair in range(DEVICES // 2):
        blocks = []
        for q in (2 * pair, 2 * pair + 1):
            sources = (q, q ^ 16, q ^ 2)
            extra = jnp.where(
                row == 0,
                tgt[sources[0] : sources[0] + 1, :],
                jnp.where(row == 1, tgt[sources[1] : sources[1] + 1, :], tgt[sources[2] : sources[2] + 1, :]),
            )
            pieces = [points(orb, s) for s in sources]
            blocks.append(jnp.concatenate([*pieces, extra], axis=1))
        out[16 * pair : 16 * (pair + 1), :] = jnp.concatenate(blocks, axis=0).astype(BF)


def pack(orbitals, targets):
    return pl.pallas_call(
        pack_kernel,
        out_shape=jax.ShapeDtypeStruct((DEVICES * 8, 4 * FB), BF),
        compiler_params=pltpu.CompilerParams(vmem_limit_bytes=32 * 2**20),
        name="pack",
    )(orbitals, targets.astype(F32).reshape(DEVICES, FB))


def unpack_kernel(packed, col_pair, row_pair):
    turned = packed[:, : 3 * FB].T
    source = lax.broadcasted_iota(jnp.int32, (NB, NT), 0)
    target = lax.broadcasted_iota(jnp.int32, (NB, NT), 1)
    for i, spots in enumerate((((col_pair, 0), (row_pair, 0)), ((col_pair, 1),), ((row_pair, 1),))):
        chosen = jnp.where(source == 8 * target + i, 1.0, 0.0).astype(BF)
        tgt = tn(packed[:, 3 * FB :], chosen).astype(BF)
        for out, side in spots:
            out[side, :, :NB] = turned[i * FB : (i + 1) * FB]
            out[side, :, NB:] = tgt


def unpack(packed):
    return pl.pallas_call(
        unpack_kernel,
        out_shape=[jax.ShapeDtypeStruct((2, FB, WIDE), BF)] * 2,
        compiler_params=pltpu.CompilerParams(vmem_limit_bytes=32 * 2**20),
        name="unpack",
    )(packed)


def cut_kernel(*refs):
    for i, (pair, out) in enumerate(zip(refs[:4], refs[4:])):
        out[...] = pair[i % 2]


def cut(*pairs):
    return pl.pallas_call(
        cut_kernel,
        out_shape=[jax.ShapeDtypeStruct((FB, WIDE), BF)] * 4,
        compiler_params=pltpu.CompilerParams(vmem_limit_bytes=16 * 2**20),
        name="cut",
    )(*pairs)


def tile_kernel(me, *refs):
    row_refs, col_refs, (kern, owned, mirrored), refs = refs[:10], refs[10:15], refs[15:18], refs[18:]
    row_own, row_other, c0, c1, c2, c3, cols, rows, stored, col_sum, sems = refs
    y, xh, z, xl, k = (me[i] for i in range(5))
    count = [0]

    def start(src, dst):
        copy = pltpu.make_async_copy(src, dst, sems.at[count[0]])
        count[0] += 1
        copy.start()
        return copy

    def block(y_step, side):
        return lax.rem(y + y_step, 4) * 2 + lax.rem(xh + side, 2)

    def place(t, b):
        return lax.rem(z + t, 4), lax.rem(xl + b % 2, 2), lax.rem(k + b // 2, 2)

    def row_copies(t):
        if t == 2:
            return [start(row_refs[4 + b], rows.at[t, b]) for b in range(4)]
        at = (0, 2, 0, 8)[t]
        return [start(row_refs[at + b], rows.at[t, pl.ds(2 * b, 2)]) for b in range(2)]

    def kern_copies(t):
        return [start(kern.at[place(t, b)], stored.at[t % 2, b]) for b in range(4)]

    first_copies = [start(col_refs[i].at[b], cols.at[block(step, b)]) for i, step in enumerate((0, 1, 3)) for b in (0, 1)]
    first_copies += [start(col_refs[3 + b], cols.at[block(2, b)]) for b in (0, 1)] + row_copies(0)
    next_rows, next_kern = [], kern_copies(0)
    col_sum[...] = jnp.zeros_like(col_sum)
    for copy in first_copies:
        copy.wait()
    col_wide = cols[...].reshape(COL_PTS, WIDE)

    for t in range(4):
        for copy in next_rows:
            copy.wait()
        kern_here = next_kern
        if t < 3:
            next_rows, next_kern = row_copies(t + 1), kern_copies(t + 1)
        row_wide = rows[t].reshape(TILE, WIDE)
        if t > 0:
            for copy in kern_here:
                copy.wait()
        gram = nt(row_wide[:, :NB], col_wide[:, :NB])
        if t == 0:
            for copy in kern_here:
                copy.wait()
        chunks = COL_PTS // 128
        values = jnp.concatenate(
            [
                jnp.concatenate([stored[t % 2, b, pl.ds(j, FB, stride=chunks), :] for j in range(chunks)], axis=1)
                for b in range(4)
            ],
            axis=0,
        )

        def spread(ref):
            return jnp.concatenate([jnp.broadcast_to(ref[place(t, b)], (FB, COL_PTS)) for b in range(4)], axis=0)

        weighted = gram * values * spread(owned)
        high = weighted.astype(BF)
        low = (weighted - high.astype(F32)).astype(BF)
        row_sum = nn(high, col_wide[:, NB:]) + nn(low, col_wide[:, NB:])
        if t == 0:
            keep = spread(mirrored).astype(BF)
            high, low = high * keep, low * keep
        added = tn(high, row_wide[:, NB:]) + tn(low, row_wide[:, NB:])
        col_sum[...] += added.reshape(col_sum.shape)
        row_own[t] = row_sum[: 2 * FB]
        row_other[t] = row_sum[2 * FB :]

    for step, col_out in enumerate((c0, c1, c2, c3)):
        for side in (0, 1):
            col_out[side * FB : (side + 1) * FB, :] = col_sum[block(step, side)]


def tile_call(me, row_parts, col_parts, kern, owned, mirrored):
    vmem = pl.BlockSpec(memory_space=pltpu.VMEM)
    hbm = pl.BlockSpec(memory_space=pltpu.HBM)
    return pl.pallas_call(
        tile_kernel,
        in_specs=[pl.BlockSpec(memory_space=pltpu.SMEM)] + [hbm] * 16 + [vmem] * 2,
        out_specs=[vmem] * 6,
        out_shape=[jax.ShapeDtypeStruct((4, 2 * FB, NT), F32)] * 2 + [jax.ShapeDtypeStruct((2 * FB, NT), F32)] * 4,
        scratch_shapes=[
            pltpu.VMEM((N_ROW, FB, WIDE), BF),
            pltpu.VMEM((4, 4, FB, WIDE), BF),
            pltpu.VMEM((2, 4, FB * COL_PTS // 128, 128), F32),
            pltpu.VMEM((N_ROW, FB, NT), F32),
            pltpu.SemaphoreType.DMA((40,)),
        ],
        compiler_params=pltpu.CompilerParams(vmem_limit_bytes=52 * 2**20),
        cost_estimate=pl.CostEstimate(flops=10_000_000_000, bytes_accessed=24_000_000, transcendentals=0),
        name="tiles",
    )(me, *row_parts, *col_parts, kern, owned, mirrored)


def local(orbitals, targets, kernel, tile_owner):
    r, c = lax.axis_index("row"), lax.axis_index("col")
    me = jnp.stack([r // 2, r % 2, c // 4, c // 2 % 2, c % 2]).astype(jnp.int32)

    packed = pack(orbitals, targets).reshape(DEVICES, 8, 4 * FB)
    packed = lax.all_to_all(packed, AXES, split_axis=0, concat_axis=0, tiled=True)
    col_pair, row_pair = unpack(packed.reshape(DEVICES * 8, 4 * FB))

    y_down, y_up = send(col_pair, y=1), send(col_pair, y=3)
    z_down, z_up = send(row_pair, z=1), send(row_pair, z=3)
    parts = cut(y_down, y_up, z_down, z_up)
    y_far, y_far_side = send(parts[0], y=1), send(parts[1], y=3)
    z_far, z_far_side = send(parts[2], z=1), send(parts[3], z=3)
    col_parts = (col_pair, y_up, y_down, y_far, y_far_side)
    row_parts = (row_pair, send(row_pair, k=1), z_up, send(z_up, k=1))
    row_parts += (z_far, z_far_side, send(z_far, k=1), send(z_far_side, k=1), z_down, send(z_down, k=1))

    flags = tile_owner.reshape(N_COL, N_ROW).astype(F32)
    here = (lax.broadcasted_iota(jnp.int32, flags.shape, 0) == c) & (
        lax.broadcasted_iota(jnp.int32, flags.shape, 1) == r
    )
    owned = jnp.repeat(flags, FB, axis=1).reshape(4, 2, 2, 1, COL_PTS)
    mirrored = jnp.repeat(jnp.where(here, 0.0, flags), FB, axis=1).reshape(4, 2, 2, 1, COL_PTS)
    kern = kernel.reshape(4, 2, 2, FB * COL_PTS // 128, 128)

    row_own, row_other, c0, c1, c2, c3 = tile_call(me, row_parts, col_parts, kern, owned, mirrored)

    col_sum = c0 + send(c2, y=2) + send(c1, y=1) + send(c3, y=3)
    row_sum = row_own + send(row_other, k=1)
    row_sum = row_sum[0] + send(row_sum[2], z=2) + send(row_sum[1], z=1) + send(row_sum[3], z=3)
    row_share = row_sum[:FB] + send(row_sum[FB:], xl=1)
    col_share = col_sum[:FB] + send(col_sum[FB:], xh=1)
    return row_share + col_share


def solution(mesh):
    in_specs = (
        P(("row", "col"), None),
        P(("row", "col"), None),
        P("row", "col", None),
        P("row", None, None, "col"),
    )
    out_specs = P(("row", "col"), None)
    return jax.shard_map(local, mesh=mesh, in_specs=in_specs, out_specs=out_specs, check_vma=False)
```

```python
import functools
import itertools

import jax
import jax.numpy as jnp
from jax import lax
from jax.experimental import pallas as pl
from jax.experimental.pallas import tpu as pltpu
from jax.sharding import PartitionSpec as P

N_ROW, N_COL, FB, NB, NT = 8, 16, 160, 1024, 128
DEVICES = N_ROW * N_COL
ROW_PTS, COL_PTS = N_COL * FB, N_ROW * FB
WIDE = NB + NT
AXES = ("row", "col")
PARTS = {"y": 4, "xh": 2, "z": 4, "xl": 2, "k": 2}
TILE = 4 * FB
BF, F32 = jnp.bfloat16, jnp.float32


def index_of(y, xh, z, xl, k):
    return (y * 2 + xh) * N_COL + z * 4 + xl * 2 + k


def moved(**steps):
    pairs = []
    for at in itertools.product(*map(range, PARTS.values())):
        to = [(a + steps.get(name, 0)) % size for a, (name, size) in zip(at, PARTS.items())]
        pairs.append((index_of(*at), index_of(*to)))
    return pairs


def send(x, **steps):
    return lax.ppermute(x, AXES, moved(**steps))


def nn(a, b):
    return jnp.dot(a, b, preferred_element_type=F32)


def nt(a, b):
    return lax.dot_general(a, b, (((1,), (1,)), ((), ())), preferred_element_type=F32)


def tn(a, b):
    return lax.dot_general(a, b, (((0,), (0,)), ((), ())), preferred_element_type=F32)


def points(ref, block):
    return ref[:, block * FB : (block + 1) * FB].astype(F32)


def pack_kernel(orb, tgt, out):
    row = lax.broadcasted_iota(jnp.int32, (8, FB), 0)
    for pair in range(DEVICES // 2):
        blocks = []
        for q in (2 * pair, 2 * pair + 1):
            sources = (q, q ^ 16, q ^ 2)
            extra = jnp.where(
                row == 0,
                tgt[sources[0] : sources[0] + 1, :],
                jnp.where(row == 1, tgt[sources[1] : sources[1] + 1, :], tgt[sources[2] : sources[2] + 1, :]),
            )
            pieces = [points(orb, s) for s in sources]
            blocks.append(jnp.concatenate([*pieces, extra], axis=1))
        out[16 * pair : 16 * (pair + 1), :] = jnp.concatenate(blocks, axis=0).astype(BF)


def pack(orbitals, targets):
    return pl.pallas_call(
        pack_kernel,
        out_shape=jax.ShapeDtypeStruct((DEVICES * 8, 4 * FB), BF),
        compiler_params=pltpu.CompilerParams(vmem_limit_bytes=32 * 2**20),
        name="pack",
    )(orbitals, targets.astype(F32).reshape(DEVICES, FB))


def unpack_kernel(packed, col_pair, row_pair):
    turned = packed[:, : 3 * FB].T
    source = lax.broadcasted_iota(jnp.int32, (NB, NT), 0)
    target = lax.broadcasted_iota(jnp.int32, (NB, NT), 1)
    for i, spots in enumerate((((col_pair, 0), (row_pair, 0)), ((col_pair, 1),), ((row_pair, 1),))):
        chosen = jnp.where(source == 8 * target + i, 1.0, 0.0).astype(BF)
        tgt = tn(packed[:, 3 * FB :], chosen).astype(BF)
        for out, side in spots:
            out[side, :, :NB] = turned[i * FB : (i + 1) * FB]
            out[side, :, NB:] = tgt


def unpack(packed):
    return pl.pallas_call(
        unpack_kernel,
        out_shape=[jax.ShapeDtypeStruct((2, FB, WIDE), BF)] * 2,
        compiler_params=pltpu.CompilerParams(vmem_limit_bytes=32 * 2**20),
        name="unpack",
    )(packed)


def cut_kernel(*refs):
    for i, (pair, out) in enumerate(zip(refs[:2], refs[2:])):
        out[...] = pair[i % 2]


def cut(*pairs):
    return pl.pallas_call(
        cut_kernel,
        out_shape=[jax.ShapeDtypeStruct((FB, WIDE), BF)] * 2,
        compiler_params=pltpu.CompilerParams(vmem_limit_bytes=16 * 2**20),
        name="cut",
    )(*pairs)


def tile_kernel(z_steps, me, *refs):
    tiles, last = len(z_steps), len(z_steps) == 1
    row_refs, refs = refs[: 2 * tiles], refs[2 * tiles :]
    col_refs, (kern, owned, mirrored), refs = refs[:5], refs[5:8], refs[8:]
    if last:
        (near_own, near_other, col_in), refs = refs[:3], refs[3:]
    row_own, row_other, *col_outs, cols, rows, stored, col_sum, sems = refs
    y, xh, z, xl, k = (me[i] for i in range(5))
    count = [0]

    def start(src, dst):
        copy = pltpu.make_async_copy(src, dst, sems.at[count[0]])
        count[0] += 1
        copy.start()
        return copy

    def block(y_step, side):
        return lax.rem(y + y_step, 4) * 2 + lax.rem(xh + side, 2)

    def place(t, b):
        return lax.rem(z + z_steps[t], 4), lax.rem(xl + b % 2, 2), lax.rem(k + b // 2, 2)

    def row_copies(t):
        return [start(row_refs[2 * t + b], rows.at[t, pl.ds(2 * b, 2)]) for b in range(2)]

    def kern_copies(t):
        return [start(kern.at[place(t, b)], stored.at[t % 2, b]) for b in range(4)]

    first_copies = [start(col_refs[i].at[b], cols.at[block(step, b)]) for i, step in enumerate((0, 1, 3)) for b in (0, 1)]
    first_copies += [start(col_refs[3 + b], cols.at[block(2, b)]) for b in (0, 1)] + row_copies(0)
    next_rows, next_kern = [], kern_copies(0)
    if last:
        col_sum[...] = col_in[...]
        for i, at in enumerate((0, 1, 3)):
            row_own[at] = near_own[i]
            row_other[at] = near_other[i]
    else:
        col_sum[...] = jnp.zeros_like(col_sum)
    for copy in first_copies:
        copy.wait()
    col_wide = cols[...].reshape(COL_PTS, WIDE)

    for t in range(tiles):
        for copy in next_rows:
            copy.wait()
        kern_here = next_kern
        if t + 1 < tiles:
            next_rows, next_kern = row_copies(t + 1), kern_copies(t + 1)
        row_wide = rows[t].reshape(TILE, WIDE)
        if t > 0:
            for copy in kern_here:
                copy.wait()
        gram = nt(row_wide[:, :NB], col_wide[:, :NB])
        if t == 0:
            for copy in kern_here:
                copy.wait()
        chunks = COL_PTS // 128
        values = jnp.concatenate(
            [
                jnp.concatenate([stored[t % 2, b, pl.ds(j, FB, stride=chunks), :] for j in range(chunks)], axis=1)
                for b in range(4)
            ],
            axis=0,
        )

        def spread(ref):
            return jnp.concatenate([jnp.broadcast_to(ref[place(t, b)], (FB, COL_PTS)) for b in range(4)], axis=0)

        weighted = gram * values * spread(owned)
        high = weighted.astype(BF)
        low = (weighted - high.astype(F32)).astype(BF)
        row_sum = nn(high, col_wide[:, NB:]) + nn(low, col_wide[:, NB:])
        if z_steps[t] == 0:
            keep = spread(mirrored).astype(BF)
            high, low = high * keep, low * keep
        added = tn(high, row_wide[:, NB:]) + tn(low, row_wide[:, NB:])
        col_sum[...] += added.reshape(col_sum.shape)
        at = 2 if last else t
        row_own[at] = row_sum[: 2 * FB]
        row_other[at] = row_sum[2 * FB :]

    if last:
        for step, col_out in enumerate(col_outs):
            for side in (0, 1):
                col_out[side * FB : (side + 1) * FB, :] = col_sum[block(step, side)]
    else:
        col_outs[0][...] = col_sum[...]


def tile_call(z_steps, me, row_parts, col_parts, kern, owned, mirrored, *before):
    tiles = len(z_steps)
    vmem = pl.BlockSpec(memory_space=pltpu.VMEM)
    hbm = pl.BlockSpec(memory_space=pltpu.HBM)
    places = 4 if before else tiles
    out_shape = [jax.ShapeDtypeStruct((places, 2 * FB, NT), F32)] * 2
    if before:
        out_shape += [jax.ShapeDtypeStruct((2 * FB, NT), F32)] * 4
    else:
        out_shape += [jax.ShapeDtypeStruct((N_ROW, FB, NT), F32)]
    return pl.pallas_call(
        functools.partial(tile_kernel, z_steps),
        in_specs=[pl.BlockSpec(memory_space=pltpu.SMEM)]
        + [hbm] * (len(row_parts) + len(col_parts) + 1)
        + [vmem] * (2 + len(before)),
        out_specs=[vmem] * len(out_shape),
        out_shape=out_shape,
        scratch_shapes=[
            pltpu.VMEM((N_ROW, FB, WIDE), BF),
            pltpu.VMEM((tiles, 4, FB, WIDE), BF),
            pltpu.VMEM((min(tiles, 2), 4, FB * COL_PTS // 128, 128), F32),
            pltpu.VMEM((N_ROW, FB, NT), F32),
            pltpu.SemaphoreType.DMA((8 + 6 * tiles,)),
        ],
        compiler_params=pltpu.CompilerParams(vmem_limit_bytes=48 * 2**20),
        cost_estimate=pl.CostEstimate(
            flops=2_600_000_000 * tiles, bytes_accessed=5_000_000 * tiles, transcendentals=0
        ),
        name="far_tile" if before else "near_tiles",
    )(me, *row_parts, *col_parts, kern, owned, mirrored, *before)


def local(orbitals, targets, kernel, tile_owner):
    r, c = lax.axis_index("row"), lax.axis_index("col")
    me = jnp.stack([r // 2, r % 2, c // 4, c // 2 % 2, c % 2]).astype(jnp.int32)

    packed = pack(orbitals, targets).reshape(DEVICES, 8, 4 * FB)
    packed = lax.all_to_all(packed, AXES, split_axis=0, concat_axis=0, tiled=True)
    col_pair, row_pair = unpack(packed.reshape(DEVICES * 8, 4 * FB))

    y_down, y_up = send(col_pair, y=1), send(col_pair, y=3)
    z_down, z_up = send(row_pair, z=1), send(row_pair, z=3)
    y_far, y_far_side = cut(y_down, y_up)
    y_far, y_far_side = send(y_far, y=1), send(y_far_side, y=3)
    col_parts = (col_pair, y_up, y_down, y_far, y_far_side)
    up_other = send(z_up, k=1)
    near_rows = (row_pair, send(row_pair, k=1), z_up, up_other, z_down, send(z_down, k=1))
    far_rows = (send(z_down, z=1), send(up_other, z=3))

    flags = tile_owner.reshape(N_COL, N_ROW).astype(F32)
    here = (lax.broadcasted_iota(jnp.int32, flags.shape, 0) == c) & (
        lax.broadcasted_iota(jnp.int32, flags.shape, 1) == r
    )
    owned = jnp.repeat(flags, FB, axis=1).reshape(4, 2, 2, 1, COL_PTS)
    mirrored = jnp.repeat(jnp.where(here, 0.0, flags), FB, axis=1).reshape(4, 2, 2, 1, COL_PTS)
    kern = kernel.reshape(4, 2, 2, FB * COL_PTS // 128, 128)

    masks = (owned, mirrored)
    near = tile_call((0, 1, 3), me, near_rows, col_parts, kern, *masks)
    row_own, row_other, c0, c1, c2, c3 = tile_call((2,), me, far_rows, col_parts, kern, *masks, *near)

    col_sum = c0 + send(c2, y=2) + send(c1, y=1) + send(c3, y=3)
    row_sum = row_own + send(row_other, k=1)
    row_sum = row_sum[0] + send(row_sum[2], z=2) + send(row_sum[1], z=1) + send(row_sum[3], z=3)
    row_share = row_sum[:FB] + send(row_sum[FB:], xl=1)
    col_share = col_sum[:FB] + send(col_sum[FB:], xh=1)
    return row_share + col_share


def solution(mesh):
    in_specs = (
        P(("row", "col"), None),
        P(("row", "col"), None),
        P("row", "col", None),
        P("row", None, None, "col"),
    )
    out_specs = P(("row", "col"), None)
    return jax.shard_map(local, mesh=mesh, in_specs=in_specs, out_specs=out_specs, check_vma=False)
```

```python
import functools
import itertools

import jax
import jax.numpy as jnp
from jax import lax
from jax.experimental import pallas as pl
from jax.experimental.pallas import tpu as pltpu
from jax.sharding import PartitionSpec as P

N_ROW, N_COL, FB, NB, NT = 8, 16, 160, 1024, 128
DEVICES = N_ROW * N_COL
ROW_PTS, COL_PTS = N_COL * FB, N_ROW * FB
WIDE = NB + NT
AXES = ("row", "col")
PARTS = {"y": 4, "xh": 2, "z": 4, "xl": 2, "k": 2}
TILE = 4 * FB
BF, F32 = jnp.bfloat16, jnp.float32


def index_of(y, xh, z, xl, k):
    return (y * 2 + xh) * N_COL + z * 4 + xl * 2 + k


def moved(**steps):
    pairs = []
    for at in itertools.product(*map(range, PARTS.values())):
        to = [(a + steps.get(name, 0)) % size for a, (name, size) in zip(at, PARTS.items())]
        pairs.append((index_of(*at), index_of(*to)))
    return pairs


def send(x, **steps):
    return lax.ppermute(x, AXES, moved(**steps))


def nn(a, b):
    return jnp.dot(a, b, preferred_element_type=F32)


def nt(a, b):
    return lax.dot_general(a, b, (((1,), (1,)), ((), ())), preferred_element_type=F32)


def tn(a, b):
    return lax.dot_general(a, b, (((0,), (0,)), ((), ())), preferred_element_type=F32)


def points(ref, block):
    return ref[:, block * FB : (block + 1) * FB].astype(F32)


def pack_kernel(orb, tgt, out):
    row = lax.broadcasted_iota(jnp.int32, (8, FB), 0)
    for pair in range(DEVICES // 2):
        blocks = []
        for q in (2 * pair, 2 * pair + 1):
            sources = (q, q ^ 16, q ^ 2)
            extra = jnp.where(
                row == 0,
                tgt[sources[0] : sources[0] + 1, :],
                jnp.where(row == 1, tgt[sources[1] : sources[1] + 1, :], tgt[sources[2] : sources[2] + 1, :]),
            )
            pieces = [points(orb, s) for s in sources]
            blocks.append(jnp.concatenate([*pieces, extra], axis=1))
        out[16 * pair : 16 * (pair + 1), :] = jnp.concatenate(blocks, axis=0).astype(BF)


def pack(orbitals, targets):
    return pl.pallas_call(
        pack_kernel,
        out_shape=jax.ShapeDtypeStruct((DEVICES * 8, 4 * FB), BF),
        compiler_params=pltpu.CompilerParams(vmem_limit_bytes=32 * 2**20),
        name="pack",
    )(orbitals, targets.astype(F32).reshape(DEVICES, FB))


def targets_of(packed, i):
    source = lax.broadcasted_iota(jnp.int32, (NB, NT), 0)
    target = lax.broadcasted_iota(jnp.int32, (NB, NT), 1)
    return tn(packed[:, 3 * FB :], jnp.where(source == 8 * target + i, 1.0, 0.0).astype(BF)).astype(BF)


def unpack_cols_kernel(packed, pair):
    turned = packed[:, : 2 * FB].T
    for side in (0, 1):
        pair[side, :, :NB] = turned[side * FB : (side + 1) * FB]
        pair[side, :, NB:] = targets_of(packed, side)


def unpack_rows_kernel(packed, col_pair, pair):
    pair[0] = col_pair[0]
    pair[1, :, :NB] = packed[:, 256:512].T[2 * FB - 256 : 3 * FB - 256]
    pair[1, :, NB:] = targets_of(packed, 2)


def unpack(kernel, name, *args):
    return pl.pallas_call(
        kernel,
        out_shape=jax.ShapeDtypeStruct((2, FB, WIDE), BF),
        compiler_params=pltpu.CompilerParams(vmem_limit_bytes=32 * 2**20),
        name=name,
    )(*args)


def cut_kernel(*refs):
    for i, (pair, out) in enumerate(zip(refs[:2], refs[2:])):
        out[...] = pair[i % 2]


def cut(*pairs):
    return pl.pallas_call(
        cut_kernel,
        out_shape=[jax.ShapeDtypeStruct((FB, WIDE), BF)] * 2,
        compiler_params=pltpu.CompilerParams(vmem_limit_bytes=16 * 2**20),
        name="cut",
    )(*pairs)


def tile_kernel(z_steps, me, *refs):
    tiles, last = len(z_steps), len(z_steps) == 1
    row_refs, refs = refs[: 2 * tiles], refs[2 * tiles :]
    col_refs, (kern, owned, mirrored), refs = refs[:5], refs[5:8], refs[8:]
    if last:
        (near_own, near_other, col_in), refs = refs[:3], refs[3:]
    row_own, row_other, *col_outs, cols, rows, stored, col_sum, sems = refs
    y, xh, z, xl, k = (me[i] for i in range(5))
    count = [0]

    def start(src, dst):
        copy = pltpu.make_async_copy(src, dst, sems.at[count[0]])
        count[0] += 1
        copy.start()
        return copy

    def block(y_step, side):
        return lax.rem(y + y_step, 4) * 2 + lax.rem(xh + side, 2)

    def place(t, b):
        return lax.rem(z + z_steps[t], 4), lax.rem(xl + b % 2, 2), lax.rem(k + b // 2, 2)

    def row_copies(t):
        return [start(row_refs[2 * t + b], rows.at[t, pl.ds(2 * b, 2)]) for b in range(2)]

    def kern_copies(t):
        return [start(kern.at[place(t, b)], stored.at[t % 2, b]) for b in range(4)]

    first_copies = [start(col_refs[i].at[b], cols.at[block(step, b)]) for i, step in enumerate((0, 1, 3)) for b in (0, 1)]
    first_copies += [start(col_refs[3 + b], cols.at[block(2, b)]) for b in (0, 1)] + row_copies(0)
    next_rows, next_kern = [], kern_copies(0)
    if last:
        col_sum[...] = col_in[...]
        for i, at in enumerate((0, 1, 3)):
            row_own[at] = near_own[i]
            row_other[at] = near_other[i]
    else:
        col_sum[...] = jnp.zeros_like(col_sum)
    for copy in first_copies:
        copy.wait()
    col_wide = cols[...].reshape(COL_PTS, WIDE)

    for t in range(tiles):
        for copy in next_rows:
            copy.wait()
        kern_here = next_kern
        if t + 1 < tiles:
            next_rows, next_kern = row_copies(t + 1), kern_copies(t + 1)
        row_wide = rows[t].reshape(TILE, WIDE)
        if t > 0:
            for copy in kern_here:
                copy.wait()
        gram = nt(row_wide[:, :NB], col_wide[:, :NB])
        if t == 0:
            for copy in kern_here:
                copy.wait()
        chunks = COL_PTS // 128
        values = jnp.concatenate(
            [
                jnp.concatenate([stored[t % 2, b, pl.ds(j, FB, stride=chunks), :] for j in range(chunks)], axis=1)
                for b in range(4)
            ],
            axis=0,
        )

        def spread(ref):
            return jnp.concatenate([jnp.broadcast_to(ref[place(t, b)], (FB, COL_PTS)) for b in range(4)], axis=0)

        weighted = gram * values * spread(owned)
        high = weighted.astype(BF)
        low = (weighted - high.astype(F32)).astype(BF)
        row_sum = nn(high, col_wide[:, NB:]) + nn(low, col_wide[:, NB:])
        if z_steps[t] == 0:
            keep = spread(mirrored).astype(BF)
            high, low = high * keep, low * keep
        added = tn(high, row_wide[:, NB:]) + tn(low, row_wide[:, NB:])
        col_sum[...] += added.reshape(col_sum.shape)
        at = 2 if last else t
        row_own[at] = row_sum[: 2 * FB]
        row_other[at] = row_sum[2 * FB :]

    if last:
        for step, col_out in enumerate(col_outs):
            for side in (0, 1):
                col_out[side * FB : (side + 1) * FB, :] = col_sum[block(step, side)]
    else:
        col_outs[0][...] = col_sum[...]


def tile_call(z_steps, me, row_parts, col_parts, kern, owned, mirrored, *before):
    tiles = len(z_steps)
    vmem = pl.BlockSpec(memory_space=pltpu.VMEM)
    hbm = pl.BlockSpec(memory_space=pltpu.HBM)
    places = 4 if before else tiles
    out_shape = [jax.ShapeDtypeStruct((places, 2 * FB, NT), F32)] * 2
    if before:
        out_shape += [jax.ShapeDtypeStruct((2 * FB, NT), F32)] * 4
    else:
        out_shape += [jax.ShapeDtypeStruct((N_ROW, FB, NT), F32)]
    return pl.pallas_call(
        functools.partial(tile_kernel, z_steps),
        in_specs=[pl.BlockSpec(memory_space=pltpu.SMEM)]
        + [hbm] * (len(row_parts) + len(col_parts) + 1)
        + [vmem] * (2 + len(before)),
        out_specs=[vmem] * len(out_shape),
        out_shape=out_shape,
        scratch_shapes=[
            pltpu.VMEM((N_ROW, FB, WIDE), BF),
            pltpu.VMEM((tiles, 4, FB, WIDE), BF),
            pltpu.VMEM((min(tiles, 2), 4, FB * COL_PTS // 128, 128), F32),
            pltpu.VMEM((N_ROW, FB, NT), F32),
            pltpu.SemaphoreType.DMA((8 + 6 * tiles,)),
        ],
        compiler_params=pltpu.CompilerParams(vmem_limit_bytes=48 * 2**20),
        cost_estimate=pl.CostEstimate(
            flops=20_000_000_000 * tiles, bytes_accessed=40_000_000 * tiles, transcendentals=0
        ),
        name="far_tile" if before else "near_tiles",
    )(me, *row_parts, *col_parts, kern, owned, mirrored, *before)


def local(orbitals, targets, kernel, tile_owner):
    r, c = lax.axis_index("row"), lax.axis_index("col")
    me = jnp.stack([r // 2, r % 2, c // 4, c // 2 % 2, c % 2]).astype(jnp.int32)

    packed = pack(orbitals, targets).reshape(DEVICES, 8, 4 * FB)
    packed = lax.all_to_all(packed, AXES, split_axis=0, concat_axis=0, tiled=True)
    packed = packed.reshape(DEVICES * 8, 4 * FB)

    col_pair = unpack(unpack_cols_kernel, "unpack_cols", packed)
    y_down, y_up = send(col_pair, y=1), send(col_pair, y=3)
    row_pair = unpack(unpack_rows_kernel, "unpack_rows", packed, col_pair)
    z_down, z_up = send(row_pair, z=1), send(row_pair, z=3)
    y_far, y_far_side = cut(y_down, y_up)
    y_far, y_far_side = send(y_far, y=1), send(y_far_side, y=3)
    col_parts = (col_pair, y_up, y_down, y_far, y_far_side)
    up_other = send(z_up, k=1)
    near_rows = (row_pair, send(row_pair, k=1), z_up, up_other, z_down, send(z_down, k=1))
    far_rows = (send(z_down, z=1), send(up_other, z=3))

    flags = tile_owner.reshape(N_COL, N_ROW).astype(F32)
    here = (lax.broadcasted_iota(jnp.int32, flags.shape, 0) == c) & (
        lax.broadcasted_iota(jnp.int32, flags.shape, 1) == r
    )
    owned = jnp.repeat(flags, FB, axis=1).reshape(4, 2, 2, 1, COL_PTS)
    mirrored = jnp.repeat(jnp.where(here, 0.0, flags), FB, axis=1).reshape(4, 2, 2, 1, COL_PTS)
    kern = kernel.reshape(4, 2, 2, FB * COL_PTS // 128, 128)

    masks = (owned, mirrored)
    near = tile_call((0, 1, 3), me, near_rows, col_parts, kern, *masks)
    row_own, row_other, c0, c1, c2, c3 = tile_call((2,), me, far_rows, col_parts, kern, *masks, *near)

    col_sum = c0 + send(c2, y=2) + send(c1, y=1) + send(c3, y=3)
    row_sum = row_own + send(row_other, k=1)
    row_sum = row_sum[0] + send(row_sum[2], z=2) + send(row_sum[1], z=1) + send(row_sum[3], z=3)
    row_share = row_sum[:FB] + send(row_sum[FB:], xl=1)
    col_share = col_sum[:FB] + send(col_sum[FB:], xh=1)
    return row_share + col_share


def solution(mesh):
    in_specs = (
        P(("row", "col"), None),
        P(("row", "col"), None),
        P("row", "col", None),
        P("row", None, None, "col"),
    )
    out_specs = P(("row", "col"), None)
    return jax.shard_map(local, mesh=mesh, in_specs=in_specs, out_specs=out_specs, check_vma=False)
```

```python
import functools
import itertools

import jax
import jax.numpy as jnp
from jax import lax
from jax.experimental import pallas as pl
from jax.experimental.pallas import tpu as pltpu
from jax.sharding import PartitionSpec as P

N_ROW, N_COL, FB, NB, NT = 8, 16, 160, 1024, 128
DEVICES = N_ROW * N_COL
ROW_PTS, COL_PTS = N_COL * FB, N_ROW * FB
WIDE = NB + NT
AXES = ("row", "col")
PARTS = {"y": 4, "xh": 2, "z": 4, "xl": 2, "k": 2}
TILE = 4 * FB
BF, F32 = jnp.bfloat16, jnp.float32


def index_of(y, xh, z, xl, k):
    return (y * 2 + xh) * N_COL + z * 4 + xl * 2 + k


def moved(**steps):
    pairs = []
    for at in itertools.product(*map(range, PARTS.values())):
        to = [(a + steps.get(name, 0)) % size for a, (name, size) in zip(at, PARTS.items())]
        pairs.append((index_of(*at), index_of(*to)))
    return pairs


def send(x, **steps):
    return lax.ppermute(x, AXES, moved(**steps))


def nn(a, b):
    return jnp.dot(a, b, preferred_element_type=F32)


def nt(a, b):
    return lax.dot_general(a, b, (((1,), (1,)), ((), ())), preferred_element_type=F32)


def tn(a, b):
    return lax.dot_general(a, b, (((0,), (0,)), ((), ())), preferred_element_type=F32)


def points(ref, block):
    return ref[:, block * FB : (block + 1) * FB].astype(F32)


def pack_kernel(orb, tgt, out):
    row = lax.broadcasted_iota(jnp.int32, (8, FB), 0)
    for pair in range(DEVICES // 2):
        blocks = []
        for q in (2 * pair, 2 * pair + 1):
            sources = (q, q ^ 16, q ^ 2)
            extra = jnp.where(
                row == 0,
                tgt[sources[0] : sources[0] + 1, :],
                jnp.where(row == 1, tgt[sources[1] : sources[1] + 1, :], tgt[sources[2] : sources[2] + 1, :]),
            )
            pieces = [points(orb, s) for s in sources]
            blocks.append(jnp.concatenate([*pieces, extra], axis=1))
        out[16 * pair : 16 * (pair + 1), :] = jnp.concatenate(blocks, axis=0).astype(BF)


def pack(orbitals, targets):
    return pl.pallas_call(
        pack_kernel,
        out_shape=jax.ShapeDtypeStruct((DEVICES * 8, 4 * FB), BF),
        compiler_params=pltpu.CompilerParams(vmem_limit_bytes=32 * 2**20),
        name="pack",
    )(orbitals, targets.astype(F32).reshape(DEVICES, FB))


def targets_of(packed, i):
    source = lax.broadcasted_iota(jnp.int32, (NB, NT), 0)
    target = lax.broadcasted_iota(jnp.int32, (NB, NT), 1)
    return tn(packed[:, 3 * FB :], jnp.where(source == 8 * target + i, 1.0, 0.0).astype(BF)).astype(BF)


def unpack_cols_kernel(packed, pair):
    turned = packed[:, : 2 * FB].T
    for side in (0, 1):
        pair[side, :, :NB] = turned[side * FB : (side + 1) * FB]
        pair[side, :, NB:] = targets_of(packed, side)


def unpack_rows_kernel(packed, col_pair, pair):
    pair[0] = col_pair[0]
    pair[1, :, :NB] = packed[:, 256:512].T[2 * FB - 256 : 3 * FB - 256]
    pair[1, :, NB:] = targets_of(packed, 2)


def unpack(kernel, name, *args):
    return pl.pallas_call(
        kernel,
        out_shape=jax.ShapeDtypeStruct((2, FB, WIDE), BF),
        compiler_params=pltpu.CompilerParams(vmem_limit_bytes=32 * 2**20),
        name=name,
    )(*args)


def cut(pair, side):
    def cut_kernel(pair, out):
        out[...] = pair[side]

    return pl.pallas_call(
        cut_kernel,
        out_shape=jax.ShapeDtypeStruct((FB, WIDE), BF),
        compiler_params=pltpu.CompilerParams(vmem_limit_bytes=16 * 2**20),
        name="cut",
    )(pair)


def tile_kernel(z_steps, me, *refs):
    tiles, last = len(z_steps), len(z_steps) == 1
    row_refs, refs = refs[: 2 * tiles], refs[2 * tiles :]
    col_refs, (kern, owned, mirrored), refs = refs[:5], refs[5:8], refs[8:]
    if last:
        (near_own, near_other, col_in), refs = refs[:3], refs[3:]
    row_own, row_other, *col_outs, cols, rows, stored, col_sum, sems = refs
    y, xh, z, xl, k = (me[i] for i in range(5))
    count = [0]

    def start(src, dst):
        copy = pltpu.make_async_copy(src, dst, sems.at[count[0]])
        count[0] += 1
        copy.start()
        return copy

    def block(y_step, side):
        return lax.rem(y + y_step, 4) * 2 + lax.rem(xh + side, 2)

    def place(t, b):
        return lax.rem(z + z_steps[t], 4), lax.rem(xl + b % 2, 2), lax.rem(k + b // 2, 2)

    def row_copies(t):
        return [start(row_refs[2 * t + b], rows.at[t, pl.ds(2 * b, 2)]) for b in range(2)]

    def kern_copies(t):
        return [start(kern.at[place(t, b)], stored.at[t % 2, b]) for b in range(4)]

    first_copies = [start(col_refs[i].at[b], cols.at[block(step, b)]) for i, step in enumerate((0, 1, 3)) for b in (0, 1)]
    first_copies += [start(col_refs[3 + b], cols.at[block(2, b)]) for b in (0, 1)] + row_copies(0)
    next_rows, next_kern = [], kern_copies(0)
    if last:
        col_sum[...] = col_in[...]
        for i, at in enumerate((0, 1, 3)):
            row_own[at] = near_own[i]
            row_other[at] = near_other[i]
    else:
        col_sum[...] = jnp.zeros_like(col_sum)
    for copy in first_copies:
        copy.wait()
    col_wide = cols[...].reshape(COL_PTS, WIDE)

    for t in range(tiles):
        for copy in next_rows:
            copy.wait()
        kern_here = next_kern
        if t + 1 < tiles:
            next_rows, next_kern = row_copies(t + 1), kern_copies(t + 1)
        row_wide = rows[t].reshape(TILE, WIDE)
        if t > 0:
            for copy in kern_here:
                copy.wait()
        gram = nt(row_wide[:, :NB], col_wide[:, :NB])
        if t == 0:
            for copy in kern_here:
                copy.wait()
        chunks = COL_PTS // 128
        values = jnp.concatenate(
            [
                jnp.concatenate([stored[t % 2, b, pl.ds(j, FB, stride=chunks), :] for j in range(chunks)], axis=1)
                for b in range(4)
            ],
            axis=0,
        )

        def spread(ref):
            return jnp.concatenate([jnp.broadcast_to(ref[place(t, b)], (FB, COL_PTS)) for b in range(4)], axis=0)

        weighted = gram * values * spread(owned)
        high = weighted.astype(BF)
        low = (weighted - high.astype(F32)).astype(BF)
        row_sum = nn(high, col_wide[:, NB:]) + nn(low, col_wide[:, NB:])
        if z_steps[t] == 0:
            keep = spread(mirrored).astype(BF)
            high, low = high * keep, low * keep
        added = tn(high, row_wide[:, NB:]) + tn(low, row_wide[:, NB:])
        col_sum[...] += added.reshape(col_sum.shape)
        at = 2 if last else t
        row_own[at] = row_sum[: 2 * FB]
        row_other[at] = row_sum[2 * FB :]

    if last:
        for step, col_out in enumerate(col_outs):
            for side in (0, 1):
                col_out[side * FB : (side + 1) * FB, :] = col_sum[block(step, side)]
    else:
        col_outs[0][...] = col_sum[...]


def tile_call(z_steps, me, row_parts, col_parts, kern, owned, mirrored, *before):
    tiles = len(z_steps)
    vmem = pl.BlockSpec(memory_space=pltpu.VMEM)
    hbm = pl.BlockSpec(memory_space=pltpu.HBM)
    places = 4 if before else tiles
    out_shape = [jax.ShapeDtypeStruct((places, 2 * FB, NT), F32)] * 2
    if before:
        out_shape += [jax.ShapeDtypeStruct((2 * FB, NT), F32)] * 4
    else:
        out_shape += [jax.ShapeDtypeStruct((N_ROW, FB, NT), F32)]
    return pl.pallas_call(
        functools.partial(tile_kernel, z_steps),
        in_specs=[pl.BlockSpec(memory_space=pltpu.SMEM)]
        + [hbm] * (len(row_parts) + len(col_parts) + 1)
        + [vmem] * (2 + len(before)),
        out_specs=[vmem] * len(out_shape),
        out_shape=out_shape,
        scratch_shapes=[
            pltpu.VMEM((N_ROW, FB, WIDE), BF),
            pltpu.VMEM((tiles, 4, FB, WIDE), BF),
            pltpu.VMEM((min(tiles, 2), 4, FB * COL_PTS // 128, 128), F32),
            pltpu.VMEM((N_ROW, FB, NT), F32),
            pltpu.SemaphoreType.DMA((8 + 6 * tiles,)),
        ],
        compiler_params=pltpu.CompilerParams(vmem_limit_bytes=48 * 2**20),
        cost_estimate=pl.CostEstimate(
            flops=20_000_000_000 * tiles, bytes_accessed=40_000_000 * tiles, transcendentals=0
        ),
        name="far_tile" if before else "near_tiles",
    )(me, *row_parts, *col_parts, kern, owned, mirrored, *before)


def local(orbitals, targets, kernel, tile_owner):
    r, c = lax.axis_index("row"), lax.axis_index("col")
    me = jnp.stack([r // 2, r % 2, c // 4, c // 2 % 2, c % 2]).astype(jnp.int32)

    packed = pack(orbitals, targets).reshape(DEVICES, 8, 4 * FB)
    packed = lax.all_to_all(packed, AXES, split_axis=0, concat_axis=0, tiled=True)
    packed = packed.reshape(DEVICES * 8, 4 * FB)

    col_pair = unpack(unpack_cols_kernel, "unpack_cols", packed)
    y_down, y_up = send(col_pair, y=1), send(col_pair, y=3)
    row_pair = unpack(unpack_rows_kernel, "unpack_rows", packed, col_pair)
    z_down, z_up = send(row_pair, z=1), send(row_pair, z=3)
    y_far, y_far_side = send(cut(y_down, 0), y=1), send(cut(y_up, 1), y=3)
    col_parts = (col_pair, y_up, y_down, y_far, y_far_side)
    up_other = send(z_up, k=1)
    near_rows = (row_pair, send(row_pair, k=1), z_up, up_other, z_down, send(z_down, k=1))
    far_rows = (send(z_down, z=1), send(up_other, z=3))

    flags = tile_owner.reshape(N_COL, N_ROW).astype(F32)
    here = (lax.broadcasted_iota(jnp.int32, flags.shape, 0) == c) & (
        lax.broadcasted_iota(jnp.int32, flags.shape, 1) == r
    )
    owned = jnp.repeat(flags, FB, axis=1).reshape(4, 2, 2, 1, COL_PTS)
    mirrored = jnp.repeat(jnp.where(here, 0.0, flags), FB, axis=1).reshape(4, 2, 2, 1, COL_PTS)
    kern = kernel.reshape(4, 2, 2, FB * COL_PTS // 128, 128)

    masks = (owned, mirrored)
    near = tile_call((0, 1, 3), me, near_rows, col_parts, kern, *masks)
    row_own, row_other, c0, c1, c2, c3 = tile_call((2,), me, far_rows, col_parts, kern, *masks, *near)

    col_sum = c0 + send(c2, y=2) + send(c1, y=1) + send(c3, y=3)
    row_sum = row_own + send(row_other, k=1)
    row_sum = row_sum[0] + send(row_sum[2], z=2) + send(row_sum[1], z=1) + send(row_sum[3], z=3)
    row_share = row_sum[:FB] + send(row_sum[FB:], xl=1)
    col_share = col_sum[:FB] + send(col_sum[FB:], xh=1)
    return row_share + col_share


def solution(mesh):
    in_specs = (
        P(("row", "col"), None),
        P(("row", "col"), None),
        P("row", "col", None),
        P("row", None, None, "col"),
    )
    out_specs = P(("row", "col"), None)
    return jax.shard_map(local, mesh=mesh, in_specs=in_specs, out_specs=out_specs, check_vma=False)
```

```python
import functools
import itertools

import jax
import jax.numpy as jnp
from jax import lax
from jax.experimental import pallas as pl
from jax.experimental.pallas import tpu as pltpu
from jax.sharding import PartitionSpec as P

N_ROW, N_COL, FB, NB, NT = 8, 16, 160, 1024, 128
DEVICES = N_ROW * N_COL
ROW_PTS, COL_PTS = N_COL * FB, N_ROW * FB
WIDE = NB + NT
AXES = ("row", "col")
PARTS = {"y": 4, "xh": 2, "z": 4, "xl": 2, "k": 2}
TILE = 4 * FB
BF, F32 = jnp.bfloat16, jnp.float32


def index_of(y, xh, z, xl, k):
    return (y * 2 + xh) * N_COL + z * 4 + xl * 2 + k


def moved(**steps):
    pairs = []
    for at in itertools.product(*map(range, PARTS.values())):
        to = [(a + steps.get(name, 0)) % size for a, (name, size) in zip(at, PARTS.items())]
        pairs.append((index_of(*at), index_of(*to)))
    return pairs


def send(x, **steps):
    return lax.ppermute(x, AXES, moved(**steps))


def nn(a, b):
    return jnp.dot(a, b, preferred_element_type=F32)


def nt(a, b):
    return lax.dot_general(a, b, (((1,), (1,)), ((), ())), preferred_element_type=F32)


def tn(a, b):
    return lax.dot_general(a, b, (((0,), (0,)), ((), ())), preferred_element_type=F32)


def points(ref, block):
    return ref[:, block * FB : (block + 1) * FB].astype(F32)


def pack_kernel(orb, tgt, out):
    row = lax.broadcasted_iota(jnp.int32, (8, FB), 0)
    for pair in range(DEVICES // 2):
        blocks = []
        for q in (2 * pair, 2 * pair + 1):
            sources = (q, q ^ 16, q ^ 2)
            extra = jnp.where(
                row == 0,
                tgt[sources[0] : sources[0] + 1, :],
                jnp.where(row == 1, tgt[sources[1] : sources[1] + 1, :], tgt[sources[2] : sources[2] + 1, :]),
            )
            pieces = [points(orb, s) for s in sources]
            blocks.append(jnp.concatenate([*pieces, extra], axis=1))
        out[16 * pair : 16 * (pair + 1), :] = jnp.concatenate(blocks, axis=0).astype(BF)


def pack(orbitals, targets):
    return pl.pallas_call(
        pack_kernel,
        out_shape=jax.ShapeDtypeStruct((DEVICES * 8, 4 * FB), BF),
        compiler_params=pltpu.CompilerParams(vmem_limit_bytes=32 * 2**20),
        name="pack",
    )(orbitals, targets.astype(F32).reshape(DEVICES, FB))


def targets_of(packed, i):
    source = lax.broadcasted_iota(jnp.int32, (NB, NT), 0)
    target = lax.broadcasted_iota(jnp.int32, (NB, NT), 1)
    return tn(packed[:, 3 * FB :], jnp.where(source == 8 * target + i, 1.0, 0.0).astype(BF)).astype(BF)


def unpack_cols_kernel(packed, pair):
    turned = packed[:, : 2 * FB].T
    for side in (0, 1):
        pair[side, :, :NB] = turned[side * FB : (side + 1) * FB]
        pair[side, :, NB:] = targets_of(packed, side)


def unpack_rows_kernel(packed, col_pair, pair):
    pair[0] = col_pair[0]
    pair[1, :, :NB] = packed[:, 256:512].T[2 * FB - 256 : 3 * FB - 256]
    pair[1, :, NB:] = targets_of(packed, 2)


def unpack(kernel, name, *args):
    return pl.pallas_call(
        kernel,
        out_shape=jax.ShapeDtypeStruct((2, FB, WIDE), BF),
        compiler_params=pltpu.CompilerParams(vmem_limit_bytes=32 * 2**20),
        name=name,
    )(*args)


def cut(pair, side):
    def cut_kernel(pair, out):
        out[...] = pair[side]

    return pl.pallas_call(
        cut_kernel,
        out_shape=jax.ShapeDtypeStruct((FB, WIDE), BF),
        compiler_params=pltpu.CompilerParams(vmem_limit_bytes=16 * 2**20),
        name="cut",
    )(pair)


def tile_kernel(z_steps, me, *refs):
    tiles, last = len(z_steps), len(z_steps) == 1
    row_refs, refs = refs[: 2 * tiles], refs[2 * tiles :]
    col_refs, (kern, owned, mirrored), refs = refs[:5], refs[5:8], refs[8:]
    if last:
        (near_own, near_other, col_in), refs = refs[:3], refs[3:]
    row_own, row_other, *col_outs, cols, rows, stored, col_sum, sems = refs
    y, xh, z, xl, k = (me[i] for i in range(5))
    count = [0]

    def start(src, dst):
        copy = pltpu.make_async_copy(src, dst, sems.at[count[0]])
        count[0] += 1
        copy.start()
        return copy

    def block(y_step, side):
        return lax.rem(y + y_step, 4) * 2 + lax.rem(xh + side, 2)

    def place(t, b):
        return lax.rem(z + z_steps[t], 4), lax.rem(xl + b % 2, 2), lax.rem(k + b // 2, 2)

    def row_copies(t):
        return [start(row_refs[2 * t + b], rows.at[t, pl.ds(2 * b, 2)]) for b in range(2)]

    def kern_copies(t):
        return [start(kern.at[place(t, b)], stored.at[t % 2, b]) for b in range(4)]

    first_copies = [start(col_refs[i].at[b], cols.at[block(step, b)]) for i, step in enumerate((0, 1, 3)) for b in (0, 1)]
    first_copies += [start(col_refs[3 + b], cols.at[block(2, b)]) for b in (0, 1)] + row_copies(0)
    if last:
        col_sum[...] = col_in[...]
        for i, at in enumerate((0, 1, 3)):
            row_own[at] = near_own[i]
            row_other[at] = near_other[i]
    else:
        col_sum[...] = jnp.zeros_like(col_sum)
    for copy in first_copies:
        copy.wait()
    next_rows, next_kern = [], kern_copies(0)
    col_wide = cols[...].reshape(COL_PTS, WIDE)

    for t in range(tiles):
        for copy in next_rows:
            copy.wait()
        kern_here = next_kern
        if t + 1 < tiles:
            next_rows, next_kern = row_copies(t + 1), kern_copies(t + 1)
        row_wide = rows[t].reshape(TILE, WIDE)
        if t > 0:
            for copy in kern_here:
                copy.wait()
        gram = nt(row_wide[:, :NB], col_wide[:, :NB])
        if t == 0:
            for copy in kern_here:
                copy.wait()
        chunks = COL_PTS // 128
        values = jnp.concatenate(
            [
                jnp.concatenate([stored[t % 2, b, pl.ds(j, FB, stride=chunks), :] for j in range(chunks)], axis=1)
                for b in range(4)
            ],
            axis=0,
        )

        def spread(ref):
            return jnp.concatenate([jnp.broadcast_to(ref[place(t, b)], (FB, COL_PTS)) for b in range(4)], axis=0)

        weighted = gram * values * spread(owned)
        high = weighted.astype(BF)
        low = (weighted - high.astype(F32)).astype(BF)
        row_sum = nn(high, col_wide[:, NB:]) + nn(low, col_wide[:, NB:])
        if z_steps[t] == 0:
            keep = spread(mirrored).astype(BF)
            high, low = high * keep, low * keep
        added = tn(high, row_wide[:, NB:]) + tn(low, row_wide[:, NB:])
        col_sum[...] += added.reshape(col_sum.shape)
        at = 2 if last else t
        row_own[at] = row_sum[: 2 * FB]
        row_other[at] = row_sum[2 * FB :]

    if last:
        for step, col_out in enumerate(col_outs):
            for side in (0, 1):
                col_out[side * FB : (side + 1) * FB, :] = col_sum[block(step, side)]
    else:
        col_outs[0][...] = col_sum[...]


def tile_call(z_steps, me, row_parts, col_parts, kern, owned, mirrored, *before):
    tiles = len(z_steps)
    vmem = pl.BlockSpec(memory_space=pltpu.VMEM)
    hbm = pl.BlockSpec(memory_space=pltpu.HBM)
    places = 4 if before else tiles
    out_shape = [jax.ShapeDtypeStruct((places, 2 * FB, NT), F32)] * 2
    if before:
        out_shape += [jax.ShapeDtypeStruct((2 * FB, NT), F32)] * 4
    else:
        out_shape += [jax.ShapeDtypeStruct((N_ROW, FB, NT), F32)]
    return pl.pallas_call(
        functools.partial(tile_kernel, z_steps),
        in_specs=[pl.BlockSpec(memory_space=pltpu.SMEM)]
        + [hbm] * (len(row_parts) + len(col_parts) + 1)
        + [vmem] * (2 + len(before)),
        out_specs=[vmem] * len(out_shape),
        out_shape=out_shape,
        scratch_shapes=[
            pltpu.VMEM((N_ROW, FB, WIDE), BF),
            pltpu.VMEM((tiles, 4, FB, WIDE), BF),
            pltpu.VMEM((min(tiles, 2), 4, FB * COL_PTS // 128, 128), F32),
            pltpu.VMEM((N_ROW, FB, NT), F32),
            pltpu.SemaphoreType.DMA((8 + 6 * tiles,)),
        ],
        compiler_params=pltpu.CompilerParams(vmem_limit_bytes=48 * 2**20),
        cost_estimate=pl.CostEstimate(
            flops=20_000_000_000 * tiles, bytes_accessed=40_000_000 * tiles, transcendentals=0
        ),
        name="far_tile" if before else "near_tiles",
    )(me, *row_parts, *col_parts, kern, owned, mirrored, *before)


def local(orbitals, targets, kernel, tile_owner):
    r, c = lax.axis_index("row"), lax.axis_index("col")
    me = jnp.stack([r // 2, r % 2, c // 4, c // 2 % 2, c % 2]).astype(jnp.int32)

    packed = pack(orbitals, targets).reshape(DEVICES, 8, 4 * FB)
    packed = lax.all_to_all(packed, AXES, split_axis=0, concat_axis=0, tiled=True)
    packed = packed.reshape(DEVICES * 8, 4 * FB)

    col_pair = unpack(unpack_cols_kernel, "unpack_cols", packed)
    y_down, y_up = send(col_pair, y=1), send(col_pair, y=3)
    row_pair = unpack(unpack_rows_kernel, "unpack_rows", packed, col_pair)
    z_down, z_up = send(row_pair, z=1), send(row_pair, z=3)
    y_far, y_far_side = send(cut(y_down, 0), y=1), send(cut(y_up, 1), y=3)
    col_parts = (col_pair, y_up, y_down, y_far, y_far_side)
    up_other = send(z_up, k=1)
    near_rows = (row_pair, send(row_pair, k=1), z_up, up_other, z_down, send(z_down, k=1))
    far_rows = (send(z_down, z=1), send(up_other, z=3))

    flags = tile_owner.reshape(N_COL, N_ROW).astype(F32)
    here = (lax.broadcasted_iota(jnp.int32, flags.shape, 0) == c) & (
        lax.broadcasted_iota(jnp.int32, flags.shape, 1) == r
    )
    owned = jnp.repeat(flags, FB, axis=1).reshape(4, 2, 2, 1, COL_PTS)
    mirrored = jnp.repeat(jnp.where(here, 0.0, flags), FB, axis=1).reshape(4, 2, 2, 1, COL_PTS)
    kern = kernel.reshape(4, 2, 2, FB * COL_PTS // 128, 128)

    masks = (owned, mirrored)
    near = tile_call((0, 1, 3), me, near_rows, col_parts, kern, *masks)
    row_own, row_other, c0, c1, c2, c3 = tile_call((2,), me, far_rows, col_parts, kern, *masks, *near)

    col_sum = c0 + send(c2, y=2) + send(c1, y=1) + send(c3, y=3)
    row_sum = row_own + send(row_other, k=1)
    row_sum = row_sum[0] + send(row_sum[2], z=2) + send(row_sum[1], z=1) + send(row_sum[3], z=3)
    row_share = row_sum[:FB] + send(row_sum[FB:], xl=1)
    col_share = col_sum[:FB] + send(col_sum[FB:], xh=1)
    return row_share + col_share


def solution(mesh):
    in_specs = (
        P(("row", "col"), None),
        P(("row", "col"), None),
        P("row", "col", None),
        P("row", None, None, "col"),
    )
    out_specs = P(("row", "col"), None)
    return jax.shard_map(local, mesh=mesh, in_specs=in_specs, out_specs=out_specs, check_vma=False)
```
